256 devices in a mesh: dp: 8 (over y_hi, x), mp: 32 (over z, y_lo, core).
Axes of the slice: x: 4, y: 4 (y_hi: 2, y_lo: 2; y = y_hi * 2 + y_lo), z: 8, core: 2. Of those that a mesh axis runs over, the one named last changes fastest.
Arguments:
- tokens: bfloat16 [2048, 6144], P('dp', 'mp'), may hold values from -15 to 15
- upstream: bfloat16 [2048, 6144], P('dp', 'mp'), may hold values from -6.4 to 6.4
- norm_gain: float32 [6144], replicated, may hold values from 0.1 to 1.9
- w_in: bfloat16 [6144, 12288], P(None, 'mp'), may hold values from -0.08930431 to 0.08930431
- w_out: bfloat16 [12288, 6144], P('mp'), may hold values from -0.0550287 to 0.0550287
Outputs:
- output: bfloat16 [2048, 6144], P('dp', 'mp')
- grad_tokens: bfloat16 [2048, 6144], P('dp', 'mp')
- grad_in: float32 [6144, 12288], P('dp', 'mp')
- grad_out: float32 [12288, 6144], P('mp', 'dp')
The draws below stay inside these ranges and needn't reach their ends.
All inputs are finite; a program needn't handle non-finite values.
Results may differ from the reference program's by a relative error of at most 0.019.
Values may be sent and summed in bfloat16 or wider, within the bound.
A program may use at most 128 MiB of HBM per device.

```python
import math
import jax
import jax.numpy as jnp
from jax import lax

D = 6144
FF = 12288
TOKENS = 2048
N_MP = 32


def shared_rows(key):
    return jnp.clip(jax.random.normal(key, (TOKENS, D), jnp.float32), -4.0, 4.0)


def shared_weights(key):
    inner_key = jax.random.fold_in(key, 101)
    return jnp.clip(jax.random.normal(inner_key, (D, FF), jnp.float32), -4.0, 4.0)


def draw_tokens(key, part):
    rows = shared_rows(key)
    key = jax.random.fold_in(key, 1)
    spread = 3.0
    position = jnp.arange(D, dtype=jnp.float32) / (D - 1)
    jitter = jnp.exp(jax.random.uniform(key, (D,), jnp.float32, -0.2, 0.2))
    scale = jnp.power(spread, position - 0.5) * jitter
    return (rows * scale[None, :]).astype(jnp.bfloat16)


def draw_upstream(key, part):
    rows = shared_rows(key)
    key = jax.random.fold_in(key, 2)
    noise = jnp.clip(jax.random.normal(key, (TOKENS, D), jnp.float32), -4.0, 4.0)
    mix = 0.6
    return (mix * rows + math.sqrt(1.0 - mix * mix) * noise).astype(jnp.bfloat16)


def draw_w_in(key, part):
    base = shared_weights(key)
    key = jax.random.fold_in(key, 3)
    column_shift = jnp.clip(jax.random.normal(key, (FF,), jnp.float32), -4.0, 4.0)
    rising = 0.5 + jnp.arange(D, dtype=jnp.float32) / (D - 1)
    return ((base + 0.5 * rising[:, None] * column_shift[None, :]) / math.sqrt(D)).astype(jnp.bfloat16)


def draw_w_out(key, part):
    base = shared_weights(key)
    key = jax.random.fold_in(key, 4)
    noise = jnp.clip(jax.random.normal(key, (FF, D), jnp.float32), -4.0, 4.0)
    mix = 0.6
    return ((mix * base.T + math.sqrt(1.0 - mix * mix) * noise) / math.sqrt(FF)).astype(jnp.bfloat16)


def setup_inputs(seed: int = 0) -> dict:
    keys = jax.random.split(jax.random.key(seed), 6)
    return {
        "tokens": draw_tokens(jax.random.fold_in(keys[5], 71), 0),
        "upstream": draw_upstream(jax.random.fold_in(keys[5], 71), 0),
        "norm_gain": jnp.clip(1.0 + 0.18 * jax.random.normal(keys[2], (D,), jnp.float32), 0.1, 1.9),
        "w_in": draw_w_in(jax.random.fold_in(keys[5], 71), 0),
        "w_out": draw_w_out(jax.random.fold_in(keys[5], 71), 0),
    }


def gelu_slope(value):
    cumul = 0.5 * (1.0 + lax.erf(value * 0.7071067811865476))
    dense = jnp.exp(-0.5 * value * value) * 0.3989422804014327
    return cumul + value * dense

def reference(tokens, upstream, norm_gain, w_in, w_out):
    block_width = FF // N_MP
    tokens_f = tokens.astype(jnp.float32)
    mean_row = lax.optimization_barrier(jnp.mean(tokens_f, axis=1, keepdims=True))
    centred = tokens_f - mean_row
    inv_std = lax.rsqrt(lax.optimization_barrier(jnp.mean(centred * centred, axis=1, keepdims=True)) + 1e-06)
    unit_rows = centred * inv_std
    normed = (unit_rows * norm_gain[None, :]).astype(jnp.bfloat16)
    preact = jnp.dot(normed, w_in, preferred_element_type=jnp.float32)
    hidden = jax.nn.gelu(preact, approximate=False).astype(jnp.bfloat16)

    def out_block(total, block):
        start = (block * block_width).astype(jnp.int32)
        hid_part = lax.dynamic_slice_in_dim(hidden, start, block_width, 1)
        w_part = lax.dynamic_slice_in_dim(w_out, start, block_width, 0)
        term = jnp.dot(hid_part, w_part, preferred_element_type=jnp.float32)
        return (total + term.astype(jnp.bfloat16).astype(jnp.float32), None)
    zeros_out = jnp.zeros((tokens.shape[0], D), jnp.float32)
    branch, _ = lax.scan(out_block, zeros_out, jnp.arange(N_MP, dtype=jnp.int32))
    output = (tokens_f + branch).astype(jnp.bfloat16)
    grad_hidden = lax.dot_general(upstream, w_out, (((1,), (1,)), ((), ())), preferred_element_type=jnp.float32)
    grad_preact = (grad_hidden * gelu_slope(preact)).astype(jnp.bfloat16)
    grad_out = lax.dot_general(hidden, upstream, (((0,), (0,)), ((), ())), preferred_element_type=jnp.float32)
    grad_in = lax.dot_general(normed, grad_preact, (((0,), (0,)), ((), ())), preferred_element_type=jnp.float32)

    def in_block(total, block):
        start = (block * block_width).astype(jnp.int32)
        grad_part = lax.dynamic_slice_in_dim(grad_preact, start, block_width, 1)
        w_part = lax.dynamic_slice_in_dim(w_in, start, block_width, 1)
        term = lax.dot_general(grad_part, w_part, (((1,), (1,)), ((), ())), preferred_element_type=jnp.float32)
        return (total + term.astype(jnp.bfloat16).astype(jnp.float32), None)
    grad_normed, _ = lax.scan(in_block, zeros_out, jnp.arange(N_MP, dtype=jnp.int32))
    scaled = grad_normed * norm_gain[None, :]
    inner = lax.optimization_barrier(jnp.mean(scaled * unit_rows, axis=1, keepdims=True))
    grad_ln = inv_std * (scaled - lax.optimization_barrier(jnp.mean(scaled, axis=1, keepdims=True)) - unit_rows * inner)
    grad_tokens = (upstream.astype(jnp.float32) + grad_ln).astype(jnp.bfloat16)
    return (output, grad_tokens, grad_in, grad_out)
```

```python
import functools

import jax
import jax.numpy as jnp
from jax import lax
from jax.experimental import pallas as pl
from jax.experimental.pallas import tpu as pltpu
from jax.sharding import PartitionSpec as P

MESH = pl.DeviceIdType.MESH
F32, BF16 = jnp.float32, jnp.bfloat16
D = 6144
BLK = 768
W = 192
TG = 256
FB = 384
ORDER = (0, 1, 3, 2)
LAG = 2


def gelu_parts(v):
    cumul = 0.5 * (1.0 + lax.erf(v * 0.7071067811865476))
    dense = jnp.exp(-0.5 * v * v) * 0.3989422804014327
    return cumul, dense


def split_rows(row):
    n = row.shape[1]
    hi = row.astype(BF16).astype(F32)
    mid = (row - hi).astype(BF16).astype(F32)
    low = row - hi - mid
    index = lax.broadcasted_iota(jnp.int32, (16, n), 0)
    spread = [jnp.broadcast_to(v, (16, n)) for v in (hi, mid, low)]
    zero = jnp.zeros((16, n), F32)
    out = jnp.where(
        index == 0, spread[0], jnp.where(index == 1, spread[1], jnp.where(index == 2, spread[2], zero))
    )
    return out.astype(BF16)


def column(row):
    return jnp.broadcast_to(row, (128, row.shape[1])).T


def dot(a, b):
    return jnp.dot(a, b, preferred_element_type=F32)


def dot_t(a, b):
    return lax.dot_general(a, b, (((1,), (1,)), ((), ())), preferred_element_type=F32)


def kernel(
    x_ref, u_ref, gain_ref, w_in_ref, w_out_ref,
    out_ref, gt_ref, gi_ref, go_ref,
    xt, nt, wi, wit, wo, wot, gcol, gzcol, srow,
    st, mean_s, inv_s, ps, pr, po, pre, hg,
    bp, br, rz, acc, fin, smo, smc, smy, smz, gs, gr, gso, gro,
    loc_sem, org_s, ag_r, ag_z, sib_s, sib_r, st_s, st_r, p_s, p_r, hg_s, hg_r,
    b_s, b_r, rz_s, rz_r, fin_s, fin_r, sm_s, sm_r, smz_s, smz_r, gr_s, gr_r,
):
    dp, mp = lax.axis_index("dp"), lax.axis_index("mp")
    h, q = lax.div(dp, 4), lax.rem(dp, 4)
    z, yl, c = lax.div(mp, 4), lax.rem(lax.div(mp, 2), 2), lax.rem(mp, 2)

    def dev(h_, x_, z_, y_, c_):
        return (h_ * 4 + x_, z_ * 4 + y_ * 2 + c_)

    def xo(k):
        return lax.rem(q + k, 4)

    def zo(k):
        return lax.rem(z + k, 8)

    sibling = dev(h, q, z, yl, 1 - c)
    ypart = dev(h, q, z, 1 - yl, c)
    hpart = dev(1 - h, q, z, yl, c)
    zplus, zminus = dev(h, q, zo(1), yl, c), dev(h, q, zo(7), yl, c)

    def remote(src, dst, ss, rs, to):
        return pltpu.make_async_remote_copy(
            src_ref=src, dst_ref=dst, send_sem=ss, recv_sem=rs, device_id=to, device_id_type=MESH
        )

    def wi_copy(k):
        return pltpu.make_async_copy(w_in_ref.at[pl.ds(k * BLK, BLK)], wi.at[k], loc_sem.at[k])

    def wo_copy(b):
        start = pl.multiple_of((q + 4 * b) * BLK, BLK)
        return pltpu.make_async_copy(w_out_ref.at[:, pl.ds(start, BLK)], wo.at[b], loc_sem.at[8 + b])

    for k in range(8):
        wi_copy(k).start()
    for b in range(2):
        wo_copy(b).start()

    partners = [sibling, ypart, hpart]
    partners += [dev(h, q, zo(k), yl, c) for k in range(1, 8)]
    partners += [dev(h, xo(k), z, y_, c) for k in range(1, 4) for y_ in (yl, 1 - yl)]
    barrier = pltpu.get_barrier_semaphore()
    for p in partners:
        pl.semaphore_signal(barrier, inc=1, device_id=p, device_id_type=MESH)
    pl.semaphore_wait(barrier, len(partners))

    def rows(y2, cc):
        return pl.ds(pl.multiple_of(y2 * 384 + cc * W, 64), W)

    xs = lax.rem(z, 4)
    zb = lax.div(z, 4)
    mine = (x_ref, u_ref)

    def origin(arr, other):
        to = dev(h, xs, z, 1 - yl if other else yl, c)
        return remote(
            mine[arr], xt.at[arr, q, zb, rows(yl, c)], org_s.at[arr, other], ag_r.at[arr, q, zb, yl], to
        )

    for arr in range(2):

        @pl.when(xs != q)
        def _():
            origin(arr, 0).start()

        origin(arr, 1).start()

    @pl.when(xs == q)
    def _():
        for arr in range(2):
            xt[arr, q, zb, rows(yl, c), :] = mine[arr][...]

    def group(gi):
        if isinstance(gi, int):
            return lax.rem(q + ORDER[gi], 4)
        return lax.rem(q + gi + jnp.where(gi == 2, 1, 0) - jnp.where(gi == 3, 1, 0), 4)

    def place(b):
        rb = lax.rem(z - q + 8 - 4 * b, 8)
        return rb, jnp.minimum(rb, 8 - rb)

    def ag_item(n):
        arr, gi, y2 = lax.div(n, 8), lax.rem(lax.div(n, 2), 4), lax.rem(n, 2)
        return arr, group(gi), y2

    def ag_copies(b, rb, n):
        arr, g, y2 = ag_item(n)
        piece = xt.at[arr, g, b, rows(y2, c)]
        recv = ag_r.at[arr, g, b, y2]
        up = (rb <= 2) | ((rb == 3) & (y2 == 0))
        down = (rb == 0) | (rb >= 6) | ((rb == 5) & (y2 == 1))
        local = (rb == 0) & (g == q) & (y2 == yl)
        c_up = remote(piece, piece, ag_z.at[arr, g, b, y2, 0], recv, zplus)
        c_down = remote(piece, piece, ag_z.at[arr, g, b, y2, 1], recv, zminus)
        c_sib = remote(piece, piece, sib_s.at[arr, g, b, y2], sib_r.at[arr, g, b, y2], sibling)
        return up, down, local, c_up, c_down, c_sib

    def ag_step(s, _):
        for b in range(2):
            rb, dist = place(b)
            n = s - LAG * dist

            @pl.when((n >= 0) & (n < 16))
            def _():
                up, down, local, c_up, c_down, c_sib = ag_copies(b, rb, n)

                @pl.when(jnp.logical_not(local))
                def _():
                    c_up.wait_recv()

                pl.when(up)(c_up.start)
                pl.when(down)(c_down.start)
                c_sib.start()

        return 0

    def ag_steps(lo, hi):
        lax.fori_loop(lo, hi, ag_step, 0)

    def prep_wi(b):
        for k in range(4 * b, 4 * b + 4):
            wi_copy(k).wait()

    def prep_s(lo, hi):
        for k in range(lo, hi):
            term = dot(split_rows(gain_ref[k : k + 1, :]), wi[k])
            if k == 0:
                srow[...] = term
            else:
                srow[...] += term

    def prep_wit(b):
        for t in range(2):
            part = wi[q + 4 * b, pl.ds(t * 384, 384), :]
            wit[b, :, t * 384 : (t + 1) * 384] = part.T

    def prep_wot(b):
        wo_copy(b).wait()
        for t in range(2):
            wot[b, t * 384 : (t + 1) * 384, :] = wo[b, :, t * 384 : (t + 1) * 384].T

    def prep_gain():
        for b in range(2):
            gcol[b] = column(gain_ref[pl.ds(q + 4 * b, 1), :])
        gzcol[...] = column(gain_ref[pl.ds(z, 1), :])

    ag_steps(0, 1)
    prep_wi(0)
    prep_wi(1)
    ag_steps(1, 2)
    prep_gain()
    ag_steps(2, 3)
    prep_wit(0)
    ag_steps(3, 4)
    prep_wit(1)
    ag_steps(4, 5)
    prep_wot(0)
    ag_steps(5, 6)
    prep_wot(1)
    ag_steps(6, 7)
    prep_s(0, 3)
    ag_steps(7, 8)
    prep_s(3, 6)
    ag_steps(8, 9)
    prep_s(6, 8)

    def wait_sib(arr, g):
        for b in range(2):
            for y2 in range(2):
                piece = xt.at[arr, g, b, rows(y2, 1 - c)]
                remote(piece, piece, sib_s.at[arr, g, b, y2], sib_r.at[arr, g, b, y2], sibling).wait_recv()

    def st_copy(g, k):
        return remote(st.at[q, g], st.at[q, g], st_s.at[g, k], st_r.at[g, q], dev(h, xo(k), z, yl, c))

    def stats(gi):
        g = group(gi)
        wait_sib(0, g)

        def total(i, t):
            piece = xt[0, g, lax.div(i, 4), pl.ds(pl.multiple_of(lax.rem(i, 4) * W, 64), W), :]
            return t + jnp.sum(piece.astype(F32).reshape(W // 8, 8, TG), axis=0)

        t = lax.fori_loop(0, 8, total, jnp.zeros((8, TG), F32))
        mean = jnp.broadcast_to(jnp.sum(t, axis=0, keepdims=True) * (1.0 / (2 * BLK)), (8, TG))

        def square(i, t):
            piece = xt[0, g, lax.div(i, 4), pl.ds(pl.multiple_of(lax.rem(i, 4) * W, 64), W), :]
            d = piece.astype(F32).reshape(W // 8, 8, TG) - mean[None]
            return t + jnp.sum(d * d, axis=0)

        t = lax.fori_loop(0, 8, square, jnp.zeros((8, TG), F32))
        st[q, g, 0] = mean
        st[q, g, 1] = jnp.broadcast_to(jnp.sum(t, axis=0, keepdims=True), (8, TG))
        for k in range(1, 4):
            st_copy(g, k).start()

    def p_copy(arr, gi):
        g = group(gi)
        return remote(ps.at[arr, g], pr.at[arr, q], p_s.at[arr, g], p_r.at[arr, q], dev(h, g, z, yl, c))

    def put_part(arr, gi, part):
        if gi == 0:
            po[arr] = part
        else:
            ps[arr, group(gi)] = part.astype(BF16)
            p_copy(arr, gi).start()

    def norm_part(gi):
        g = group(gi)
        for k in range(1, 4):
            other = st.at[xo(k), g]
            remote(other, other, st_s.at[g, k], st_r.at[g, xo(k)], sibling).wait_recv()
        means = [st[i, g, 0] for i in range(4)]
        mean = (means[0] + means[1] + means[2] + means[3]) * 0.25
        spread = st[0, g, 1] + st[1, g, 1] + st[2, g, 1] + st[3, g, 1]
        for m in means:
            spread = spread + (m - mean) * (m - mean) * (2.0 * BLK)
        inv = lax.rsqrt(spread / D + 1e-06)
        mean_s[g] = mean
        inv_s[g] = inv

        def scale(i, _):
            b = lax.div(i, 4)
            r = pl.ds(pl.multiple_of(lax.rem(i, 4) * W, 64), W)
            piece = xt[0, g, b, r, :].astype(F32).reshape(W // 8, 8, TG)
            unit = ((piece - mean[None]) * inv[None]).reshape(W, TG)
            gain = gcol[b, r, :]
            nt[g, b, r, :] = (unit * jnp.concatenate([gain, gain], axis=1)).astype(BF16)
            return 0

        lax.fori_loop(0, 8, scale, 0)
        put_part(0, gi, dot(wit[0], nt[g, 0]) + dot(wit[1], nt[g, 1]))

    def up_part(gi):
        g = group(gi)
        wait_sib(1, g)
        put_part(1, gi, dot(wo[0], xt[1, g, 0]) + dot(wo[1], xt[1, g, 1]))

    def summed(arr):
        total = po[arr]
        for k in range(1, 4):
            other = pr.at[arr, xo(k)]
            remote(other, other, p_s.at[arr, k], p_r.at[arr, xo(k)], sibling).wait_recv()
            total = total + pr[arr, xo(k)].astype(F32)
        return total

    def hg_copy(arr, k):
        return remote(hg.at[arr, q], hg.at[arr, q], hg_s.at[arr, k], hg_r.at[arr, q], dev(h, xo(k), z, yl, c))

    def finish_h():
        preact = summed(0)
        pre[...] = preact
        cumul, _ = gelu_parts(preact)
        hg[0, q] = (preact * cumul).astype(BF16)
        for k in range(1, 4):
            hg_copy(0, k).start()

    def sm_copy(stage):
        dst, to = ((smc, sibling), (smy, ypart))[stage]
        return remote(smo.at[stage], dst, sm_s.at[stage], sm_r.at[stage], to)

    def smz_copy(k):
        return remote(smo.at[2], smz.at[z], smz_s.at[k], smz_r.at[z], dev(h, q, zo(k), yl, c))

    def finish_g():
        grad_hidden = summed(1)
        preact = pre[...]
        cumul, dense = gelu_parts(preact)
        grad = (grad_hidden * (cumul + preact * dense)).astype(BF16)
        hg[1, q] = grad
        for k in range(1, 4):
            hg_copy(1, k).start()
        by_gain = split_rows(jnp.sum(srow[...], axis=0, keepdims=True))
        smo[0, 0] = jnp.broadcast_to(jnp.sum(dot(by_gain, grad), axis=0, keepdims=True), (8, TG))
        inner = jnp.sum(grad.astype(F32) * preact, axis=0, keepdims=True)
        smo[0, 1] = jnp.broadcast_to(inner, (8, TG))
        sm_copy(0).start()

    def small_1():
        sm_copy(0).wait_recv()
        smo[1] = smo[0] + smc[...]
        sm_copy(1).start()

    def small_2():
        sm_copy(1).wait_recv()
        smo[2] = smo[1] + smy[...]
        for k in range(1, 8):
            smz_copy(k).start()

    def b_copy(arr, g, b):
        return remote(bp.at[arr, g, b, 1 - c], br.at[arr, g, b], b_s.at[arr, g, b], b_r.at[arr, g, b], sibling)

    def back_part(arr, gi):
        g = group(gi)
        if gi:
            other = hg.at[arr, g]
            remote(other, other, hg_s.at[arr, gi], hg_r.at[arr, g], sibling).wait_recv()
        act = hg[arr, g]
        for b in range(2):
            for y2 in range(2):
                w = wot[b, y2 * 384 : (y2 + 1) * 384, :] if arr == 0 else wi[q + 4 * b, pl.ds(y2 * 384, 384), :]
                part = dot(w, act).astype(BF16)
                bp[arr, g, b, 0, y2] = part[:W]
                bp[arr, g, b, 1, y2] = part[W:]
            b_copy(arr, g, b).start()

    def rs_flags(rb, g, y2):
        from_up = (rb <= 2) | ((rb == 3) & (y2 == 0))
        from_down = (rb == 0) | (rb >= 6) | ((rb == 5) & (y2 == 1))
        to_down = ((rb >= 1) & (rb <= 3)) | ((rb == 4) & (y2 == 0))
        to_up = (rb >= 5) | ((rb == 4) & (y2 == 1))
        sink = rb == 0
        local = sink & (g == q) & (y2 == yl)
        return from_up, from_down, to_up, to_down, sink, local

    def rs_copies(b, arr, g, y2):
        piece = bp.at[arr, g, b, c, y2]
        c_down = remote(piece, rz.at[arr, g, b, y2, 0], rz_s.at[arr, g, b, y2], rz_r.at[arr, g, b, y2, 0], zminus)
        c_up = remote(piece, rz.at[arr, g, b, y2, 1], rz_s.at[arr, g, b, y2], rz_r.at[arr, g, b, y2, 1], zplus)
        c_fin = remote(piece, fin.at[arr, yl], fin_s.at[arr, g, y2], fin_r.at[arr, yl], dev(h, g, z, y2, c))
        return c_up, c_down, c_fin

    def rs_step(s, _):
        for b in range(2):
            rb, dist = place(b)
            n = s - LAG * (4 - dist)

            @pl.when((n >= 0) & (n < 16))
            def _():
                arr, g, y2 = ag_item(n)
                from_up, from_down, to_up, to_down, sink, local = rs_flags(rb, g, y2)
                c_up, c_down, c_fin = rs_copies(b, arr, g, y2)

                @pl.when(y2 == 0)
                def _():
                    b_copy(arr, g, b).wait_recv()

                acc[...] = bp[arr, g, b, c, y2].astype(F32) + br[arr, g, b, y2].astype(F32)

                @pl.when(from_up)
                def _():
                    c_down.wait_recv()
                    acc[...] += rz[arr, g, b, y2, 0].astype(F32)

                @pl.when(from_down)
                def _():
                    c_up.wait_recv()
                    acc[...] += rz[arr, g, b, y2, 1].astype(F32)

                bp[arr, g, b, c, y2] = acc[...].astype(BF16)
                pl.when(to_up)(c_up.start)
                pl.when(to_down)(c_down.start)
                pl.when(sink & jnp.logical_not(local))(c_fin.start)

                @pl.when(local)
                def _():
                    fin[arr, yl] = acc[...].astype(BF16)

        return 0

    def rs_steps(lo, hi):
        lax.fori_loop(lo, hi, rs_step, 0)

    def gr_copy(i):
        return remote((gs, gso)[i].at[0], (gr, gro)[i].at[0], gr_s.at[i], gr_r.at[i], hpart)

    def grad_out_part():
        for t in range(2):
            other = sum(dot_t(hg[0, g], xt[1, g, 1 - h, pl.ds(t * 384, 384), :]) for g in range(4))
            gso[0, :, t * 384 : (t + 1) * 384] = other.astype(BF16)
        gr_copy(1).start()
        for t in range(2):
            go_ref[:, t * 384 : (t + 1) * 384] = sum(
                dot_t(hg[0, g], xt[1, g, h, pl.ds(t * 384, 384), :]) for g in range(4)
            )

    def grad_in_part():
        for t in range(2):
            other = sum(dot_t(nt[g, 1 - h, pl.ds(t * 384, 384), :], hg[1, g]) for g in range(4))
            gs[0, t * 384 : (t + 1) * 384, :] = other.astype(BF16)
        gr_copy(0).start()
        for t in range(2):
            gi_ref[t * 384 : (t + 1) * 384, :] = sum(
                dot_t(nt[g, h, pl.ds(t * 384, 384), :], hg[1, g]) for g in range(4)
            )

    base = 4 * LAG
    ag_steps(9, base + 2)
    for i in range(4):
        stats(i)
        ag_steps(base + 2 + 2 * i, base + 4 + 2 * i)
    norm_part(1)
    up_part(0)
    norm_part(2)
    ag_steps(base + 10, base + 12)
    norm_part(3)
    up_part(1)
    norm_part(0)
    ag_steps(base + 12, base + 14)
    up_part(2)
    ag_steps(base + 14, base + 16)
    up_part(3)
    finish_h()
    back_part(0, 0)
    back_part(0, 1)
    rs_steps(0, 2)
    finish_g()
    back_part(0, 2)
    rs_steps(2, 4)
    small_1()
    back_part(0, 3)
    rs_steps(4, 6)
    grad_out_part()
    small_2()
    back_part(1, 0)
    rs_steps(6, 8)
    back_part(1, 1)
    rs_steps(8, 10)
    back_part(1, 2)
    rs_steps(10, 12)
    back_part(1, 3)
    rs_steps(12, 14)
    grad_in_part()
    rs_steps(14, base + 16)

    def fin_wait(arr):
        for y2 in range(2):

            @pl.when(jnp.logical_not((xs == q) & (yl == y2)))
            def _():
                piece = fin.at[arr, y2]
                remote(piece, piece, fin_s.at[arr, 0, y2], fin_r.at[arr, y2], sibling).wait_recv()

    fin_wait(0)
    out_ref[...] = (x_ref[...].astype(F32) + (fin[0, 0].astype(F32) + fin[0, 1].astype(F32))).astype(BF16)

    sums = smo[2]
    for k in range(1, 8):
        remote(smz.at[zo(k)], smz.at[zo(k)], smz_s.at[k], smz_r.at[zo(k)], sibling).wait_recv()
        sums = sums + smz[zo(k)]
    mean, inv = mean_s[q][None], inv_s[q][None]
    unit = (x_ref[...].astype(F32).reshape(W // 8, 8, TG) - mean) * inv
    gain = gzcol[rows(yl, c), :]
    gain = jnp.concatenate([gain, gain], axis=1)
    fin_wait(1)
    scaled = ((fin[1, 0].astype(F32) + fin[1, 1].astype(F32)) * gain).reshape(W // 8, 8, TG)
    grad_ln = inv * (scaled - (sums[0] / D)[None] - unit * (sums[1] / D)[None])
    gt_ref[...] = (u_ref[...].astype(F32) + grad_ln.reshape(W, TG)).astype(BF16)

    gr_copy(0).wait_recv()
    gi_ref[...] += gr[0].astype(F32)
    gr_copy(1).wait_recv()
    go_ref[...] += gro[0].astype(F32)

    for arr in range(2):
        pl.when(xs != q)(origin(arr, 0).wait_send)
        origin(arr, 1).wait_send()
        for k in range(1, 4):
            hg_copy(arr, k).wait_send()
            p_copy(arr, k).wait_send()
    for i in range(2):
        gr_copy(i).wait_send()
        sm_copy(i).wait_send()
    for k in range(1, 8):
        smz_copy(k).wait_send()

    def drain(n, _):
        for b in range(2):
            rb, _ = place(b)
            up, down, _, c_up, c_down, c_sib = ag_copies(b, rb, n)
            pl.when(up)(c_up.wait_send)
            pl.when(down)(c_down.wait_send)
            c_sib.wait_send()
            arr, g, y2 = ag_item(n)
            _, _, to_up, to_down, sink, local = rs_flags(rb, g, y2)
            c_up, c_down, c_fin = rs_copies(b, arr, g, y2)
            pl.when(to_up)(c_up.wait_send)
            pl.when(to_down)(c_down.wait_send)
            pl.when(sink & jnp.logical_not(local))(c_fin.wait_send)
            pl.when(y2 == 0)(b_copy(arr, g, b).wait_send)
        return 0

    lax.fori_loop(0, 16, drain, 0)

    def drain_st(g, _):
        for k in range(1, 4):
            st_copy(g, k).wait_send()
        return 0

    lax.fori_loop(0, 4, drain_st, 0)


def body(tokens, upstream, norm_gain, w_in, w_out):
    sem = pltpu.SemaphoreType.DMA
    vmem = pl.BlockSpec(memory_space=pltpu.VMEM)
    hbm = pl.BlockSpec(memory_space=pl.ANY)
    scratch = [
        pltpu.VMEM((2, 4, 2, BLK, TG), BF16),
        pltpu.VMEM((4, 2, BLK, TG), BF16),
        pltpu.VMEM((8, BLK, FB), BF16),
        pltpu.VMEM((2, FB, BLK), BF16),
        pltpu.VMEM((2, FB, BLK), BF16),
        pltpu.VMEM((2, BLK, FB), BF16),
        pltpu.VMEM((2, BLK, 128), F32),
        pltpu.VMEM((BLK, 128), F32),
        pltpu.VMEM((16, FB), F32),
        pltpu.VMEM((4, 4, 2, 8, TG), F32),
        pltpu.VMEM((4, 8, TG), F32),
        pltpu.VMEM((4, 8, TG), F32),
        pltpu.VMEM((2, 4, FB, TG), BF16),
        pltpu.VMEM((2, 4, FB, TG), BF16),
        pltpu.VMEM((2, FB, TG), F32),
        pltpu.VMEM((FB, TG), F32),
        pltpu.VMEM((2, 4, FB, TG), BF16),
        pltpu.VMEM((2, 4, 2, 2, 2, W, TG), BF16),
        pltpu.VMEM((2, 4, 2, 2, W, TG), BF16),
        pltpu.VMEM((2, 4, 2, 2, 2, W, TG), BF16),
        pltpu.VMEM((W, TG), F32),
        pltpu.VMEM((2, 2, W, TG), BF16),
        pltpu.VMEM((3, 2, 8, TG), F32),
        pltpu.VMEM((2, 8, TG), F32),
        pltpu.VMEM((2, 8, TG), F32),
        pltpu.VMEM((8, 2, 8, TG), F32),
        pltpu.VMEM((1, BLK, FB), BF16),
        pltpu.VMEM((1, BLK, FB), BF16),
        pltpu.VMEM((1, FB, BLK), BF16),
        pltpu.VMEM((1, FB, BLK), BF16),
        sem((10,)),
        sem((2, 2)),
        sem((2, 4, 2, 2)),
        sem((2, 4, 2, 2, 2)),
        sem((2, 4, 2, 2)),
        sem((2, 4, 2, 2)),
        sem((4, 4)),
        sem((4, 4)),
        sem((2, 4)),
        sem((2, 4)),
        sem((2, 4)),
        sem((2, 4)),
        sem((2, 4, 2)),
        sem((2, 4, 2)),
        sem((2, 4, 2, 2)),
        sem((2, 4, 2, 2, 2)),
        sem((2, 4, 2)),
        sem((2, 2)),
        sem((2,)),
        sem((2,)),
        sem((8,)),
        sem((8,)),
        sem((2,)),
        sem((2,)),
    ]
    out_t, grad_t, grad_in, grad_out = pl.pallas_call(
        kernel,
        out_shape=(
            jax.ShapeDtypeStruct((W, TG), BF16),
            jax.ShapeDtypeStruct((W, TG), BF16),
            jax.ShapeDtypeStruct((BLK, FB), F32),
            jax.ShapeDtypeStruct((FB, BLK), F32),
        ),
        in_specs=[vmem, vmem, vmem, hbm, hbm],
        out_specs=(vmem, vmem, vmem, vmem),
        scratch_shapes=scratch,
        compiler_params=pltpu.CompilerParams(
            collective_id=1, has_side_effects=True, vmem_limit_bytes=58 << 20
        ),
        name="block",
    )(tokens.T, upstream.T, norm_gain.reshape(8, BLK), w_in, w_out)
    return out_t.T, grad_t.T, grad_in, grad_out


def solution(mesh):
    return jax.shard_map(
        body,
        mesh=mesh,
        in_specs=(P("dp", "mp"), P("dp", "mp"), P(), P(None, "mp"), P("mp", None)),
        out_specs=(P("dp", "mp"), P("dp", "mp"), P("dp", "mp"), P("mp", "dp")),
        check_vma=False,
    )
```

```python
import functools

import jax
import jax.numpy as jnp
from jax import lax
from jax.experimental import pallas as pl
from jax.experimental.pallas import tpu as pltpu
from jax.sharding import PartitionSpec as P

MESH = pl.DeviceIdType.MESH
F32, BF16 = jnp.float32, jnp.bfloat16
D = 6144
BLK = 768
W = 192
TG = 256
FB = 384
ORDER = ((0, 2, 3, 1), (3, 1, 0, 2))
AG_ALONE = 1
RS_ALONE = 0
AG_ITEMS = 6 if AG_ALONE else 8
RS_ITEMS = 6 if RS_ALONE else 8
LAG = 2
YLAG = 2
RYLAG = 2
FILL = 4 * LAG
EXTRA = YLAG - 2 if AG_ALONE else 0
AG_END = 2 * AG_ITEMS + FILL + EXTRA
RS_START = 22
RS_END = RS_START + 2 * RS_ITEMS + FILL
LATE = 5
BACK = (0, 2, 4, 6)
GRAD_OUT = RS_START + 6
GRAD_IN = RS_START + 14


def gelu_parts(v):
    cumul = 0.5 * (1.0 + lax.erf(v * 0.7071067811865476))
    dense = jnp.exp(-0.5 * v * v) * 0.3989422804014327
    return cumul, dense


def split_rows(row):
    n = row.shape[1]
    hi = row.astype(BF16).astype(F32)
    mid = (row - hi).astype(BF16).astype(F32)
    low = row - hi - mid
    index = lax.broadcasted_iota(jnp.int32, (16, n), 0)
    spread = [jnp.broadcast_to(v, (16, n)) for v in (hi, mid, low)]
    zero = jnp.zeros((16, n), F32)
    out = jnp.where(
        index == 0, spread[0], jnp.where(index == 1, spread[1], jnp.where(index == 2, spread[2], zero))
    )
    return out.astype(BF16)


def column(row):
    return jnp.broadcast_to(row, (128, row.shape[1])).T


def dot(a, b):
    return jnp.dot(a, b, preferred_element_type=F32)


def dot_t(a, b):
    return lax.dot_general(a, b, (((1,), (1,)), ((), ())), preferred_element_type=F32)


def kernel(
    x_ref, u_ref, gain_ref, w_in_ref, w_out_ref,
    out_ref, gt_ref, gi_ref, go_ref,
    xt, nt, wi, wit, wo, wot, gcol, gzcol, srow,
    gain8, st, stm, stz, stx, ps, pr, po, pre, hg,
    bp, br, rz, ry, acc, fin, smo, smc, smy, smz, gs, gr, gso, gro, gi_own, go_own, out_own, gt_own,
    loc_sem, org_s, ag_r, ag_z, ag_y, sib_s, sib_r, st_s, st_r, stz_s, stz_r, stx_s, stx_r, p_s, p_r, hg_s, hg_r,
    b_s, b_r, rz_s, rz_r, ry_s, ry_r, fin_s, fin_r, sm_s, sm_r, smz_s, smz_r, gr_s, gr_r, out_sem,
):
    dp, mp = lax.axis_index("dp"), lax.axis_index("mp")
    h, q = lax.div(dp, 4), lax.rem(dp, 4)
    z, yl, c = lax.div(mp, 4), lax.rem(lax.div(mp, 2), 2), lax.rem(mp, 2)

    def dev(h_, x_, z_, y_, c_):
        return (h_ * 4 + x_, z_ * 4 + y_ * 2 + c_)

    def xo(k):
        return lax.rem(q + k, 4)

    def zo(k):
        return lax.rem(z + k, 8)

    sibling = dev(h, q, z, yl, 1 - c)
    ypart = dev(h, q, z, 1 - yl, c)
    hpart = dev(1 - h, q, z, yl, c)
    zplus, zminus = dev(h, q, zo(1), yl, c), dev(h, q, zo(7), yl, c)

    def remote(src, dst, ss, rs, to):
        return pltpu.make_async_remote_copy(
            src_ref=src, dst_ref=dst, send_sem=ss, recv_sem=rs, device_id=to, device_id_type=MESH
        )

    def wi_copy(k):
        return pltpu.make_async_copy(w_in_ref.at[pl.ds(k * BLK, BLK)], wi.at[k], loc_sem.at[k])

    def wo_copy(b):
        start = pl.multiple_of((q + 4 * b) * BLK, BLK)
        return pltpu.make_async_copy(w_out_ref.at[:, pl.ds(start, BLK)], wo.at[b], loc_sem.at[8 + b])

    for k in range(8):
        wi_copy(k).start()
    for b in range(2):
        wo_copy(b).start()

    partners = [sibling, ypart, hpart]
    partners += [dev(h, q, zo(k), yl, c) for k in range(1, 8)]
    partners += [dev(h, xo(k), z, y_, c) for k in range(1, 4) for y_ in (yl, 1 - yl)]
    barrier = pltpu.get_barrier_semaphore()
    for p in partners:
        pl.semaphore_signal(barrier, inc=1, device_id=p, device_id_type=MESH)
    pl.semaphore_wait(barrier, len(partners))

    def rows(y2, cc):
        return pl.ds(pl.multiple_of(y2 * 384 + cc * W, 64), W)

    xs = lax.rem(z, 4)
    zb = lax.div(z, 4)
    mine = (x_ref, u_ref)

    def own_only(k):
        return (k == 0) | (k == 3) if AG_ALONE else k < 0

    from_xs = lax.rem(q - xs + 4, 4)

    def origin(arr, other):
        to = dev(h, xs, z, 1 - yl if other else yl, c)
        return remote(
            mine[arr], xt.at[arr, q, zb, rows(yl, c)], org_s.at[arr, other], ag_r.at[arr, q, zb, yl], to
        )

    for arr in range(2):
        pl.when(xs != q)(origin(arr, 0).start)
        pl.when(jnp.logical_not(own_only(from_xs)))(origin(arr, 1).start)

    @pl.when(xs == q)
    def _():
        for arr in range(2):
            xt[arr, q, zb, rows(yl, c), :] = mine[arr][...]

    def st_copy(stage):
        return remote(st.at[stage], stm.at[stage], st_s.at[stage], st_r.at[stage], (sibling, ypart)[stage])

    def stz_copy(k):
        return remote(st.at[2], stz.at[z], stz_s.at[k], stz_r.at[z], dev(h, q, zo(k), yl, c))

    def stx_copy(k):
        return remote(stx.at[q], stx.at[q], stx_s.at[k], stx_r.at[q], dev(h, xo(k), z, yl, c))

    def own_stats():
        piece = x_ref[...].astype(F32).reshape(W // 8, 8, TG)
        total = jnp.sum(jnp.sum(piece, axis=0), axis=0, keepdims=True)
        mean = jnp.broadcast_to(total * (1.0 / W), (8, TG))
        d = piece - mean[None]
        st[0, 0] = mean
        spread = jnp.sum(jnp.sum(d * d, axis=0), axis=0, keepdims=True)
        st[0, 1] = jnp.broadcast_to(spread, (8, TG))
        st_copy(0).start()

    def merge(parts, count):
        mean = sum(p[0] for p in parts) * (1.0 / len(parts))
        spread = sum(p[1] for p in parts)
        for p in parts:
            spread = spread + (p[0] - mean) * (p[0] - mean) * float(count)
        return mean, spread

    def merge_pair(stage):
        st_copy(stage).wait_recv()
        parts = [(st[stage, 0], st[stage, 1]), (stm[stage, 0], stm[stage, 1])]
        st[stage + 1, 0], st[stage + 1, 1] = merge(parts, W * (stage + 1))
        if stage == 0:
            st_copy(1).start()
        else:
            for k in range(1, 8):
                stz_copy(k).start()

    def merge_z():
        parts = [(st[2, 0], st[2, 1])]
        for k in range(1, 8):
            other = stz.at[zo(k)]
            remote(other, other, stz_s.at[k], stz_r.at[zo(k)], sibling).wait_recv()
            parts.append((stz[zo(k), 0], stz[zo(k), 1]))
        mean, spread = merge(parts, 4 * W)
        stx[q, 0] = mean
        stx[q, 1] = lax.rsqrt(spread / D + 1e-06)
        for k in range(1, 4):
            stx_copy(k).start()

    own_stats()

    odd = lax.rem(q, 2)

    def offset(turn):
        off = [jnp.where(odd == 1, ORDER[1][i], ORDER[0][i]) for i in range(4)]
        if isinstance(turn, int):
            return off[turn]
        return jnp.where(turn < 2, jnp.where(turn == 0, off[0], off[1]), jnp.where(turn == 2, off[2], off[3]))

    def item(n, single):
        if AG_ALONE if single == 0 else RS_ALONE:
            arr, m = lax.div(n, 6), lax.rem(n, 6)
            pair, w = lax.div(m, 3), lax.rem(m, 3)
            alone = w == (0 if single == 0 else 2)
            turn = 2 * pair + jnp.where(alone, single, 1 - single)
            y2 = jnp.where(alone, yl, w - (1 if single == 0 else 0))
        else:
            arr, m = lax.div(n, 8), lax.rem(n, 8)
            turn, y2, alone = lax.div(m, 2), lax.rem(m, 2), m < 0
        return arr, xo(offset(turn)), y2, alone

    def place(b):
        rb = lax.rem(z - q + 8 - 4 * b, 8)
        return rb, jnp.minimum(rb, 8 - rb)

    def sib_copy(arr, g, b, y2, cc):
        piece = xt.at[arr, g, b, rows(y2, cc)]
        return remote(piece, piece, sib_s.at[arr, g, b, y2], sib_r.at[arr, g, b, y2], sibling)

    def ag_copies(b, rb, n):
        arr, g, y2, alone = item(n, 0)
        piece = xt.at[arr, g, b, rows(y2, c)]
        recv = ag_r.at[arr, g, b, y2]
        up = (rb <= 2) | ((rb == 3) & (y2 == 0))
        down = (rb == 0) | (rb >= 6) | ((rb == 5) & (y2 == 1))
        local = (rb == 0) & (g == q) & (y2 == yl)
        c_up = remote(piece, piece, ag_z.at[arr, g, b, y2, 0], recv, zplus)
        c_down = remote(piece, piece, ag_z.at[arr, g, b, y2, 1], recv, zminus)
        c_y = remote(piece, piece, ag_y.at[arr, g, b], recv, ypart)
        return up, down, local, alone, c_up, c_down, c_y, sib_copy(arr, g, b, y2, c)

    def ag_step(s):
        for b in range(2):
            rb, dist = place(b)
            n = s - LAG * dist

            @pl.when((n >= 0) & (n < 2 * AG_ITEMS))
            def _():
                up, down, local, alone, c_up, c_down, c_y, c_sib = ag_copies(b, rb, n)

                @pl.when(jnp.logical_not(local))
                def _():
                    c_up.wait_recv()

                pl.when(up)(c_up.start)
                pl.when(down)(c_down.start)
                pl.when(alone)(c_y.start)
                c_sib.start()

        for b in range(2):
            _, dist = place(b)
            late = s - LAG * dist - YLAG

            @pl.when((late >= 0) & (late < 2 * AG_ITEMS))
            def _():
                arr, g, _, alone = item(late, 0)

                @pl.when(alone)
                def _():
                    c_sib = sib_copy(arr, g, b, 1 - yl, c)
                    piece = xt.at[arr, g, b, rows(1 - yl, c)]
                    remote(piece, piece, ag_y.at[arr, g, b], ag_r.at[arr, g, b, 1 - yl], ypart).wait_recv()
                    c_sib.start()

    def prep_wi(b):
        for k in range(4 * b, 4 * b + 4):
            wi_copy(k).wait()

    def prep_s(lo, hi):
        for k in range(lo, hi):
            term = dot(split_rows(gain8[k : k + 1, :]), wi[k])
            if k == 0:
                srow[...] = term
            else:
                srow[...] += term

    def prep_wit(b):
        for t in range(2):
            part = wi[q + 4 * b, pl.ds(t * 384, 384), :]
            wit[b, :, t * 384 : (t + 1) * 384] = part.T

    def prep_wot(b):
        wo_copy(b).wait()
        for t in range(2):
            wot[b, t * 384 : (t + 1) * 384, :] = wo[b, :, t * 384 : (t + 1) * 384].T

    def prep_gain():
        for k in range(8):
            gain8[k : k + 1, :] = gain_ref[k * BLK : (k + 1) * BLK].reshape(1, BLK)
        for b in range(2):
            gcol[b] = column(gain8[pl.ds(q + 4 * b, 1), :])
        gzcol[...] = column(gain8[pl.ds(z, 1), :])

    def wait_sib(arr, g):
        for b in range(2):
            for y2 in range(2):
                sib_copy(arr, g, b, y2, 1 - c).wait_recv()

    def p_copy(arr, k):
        return remote(ps.at[arr, xo(k)], pr.at[arr, q], p_s.at[arr, k], p_r.at[arr, q], dev(h, xo(k), z, yl, c))

    def put_part(arr, k, part):
        @pl.when(k == 0)
        def _():
            po[arr] = part

        @pl.when(k > 0)
        def _():
            ps[arr, xo(k)] = part.astype(BF16)
            p_copy(arr, k).start()

    def norm_part(turn):
        k = offset(turn)
        g = xo(k)
        wait_sib(0, g)

        @pl.when(k > 0)
        def _():
            other = stx.at[g]
            remote(other, other, stx_s.at[k], stx_r.at[g], sibling).wait_recv()

        mean, inv = stx[g, 0], stx[g, 1]

        def scale(i, _):
            b = lax.div(i, 4)
            r = pl.ds(pl.multiple_of(lax.rem(i, 4) * W, 64), W)
            piece = xt[0, g, b, r, :].astype(F32).reshape(W // 8, 8, TG)
            unit = ((piece - mean[None]) * inv[None]).reshape(W, TG)
            gain = gcol[b, r, :]
            nt[g, b, r, :] = (unit * jnp.concatenate([gain, gain], axis=1)).astype(BF16)
            return 0

        lax.fori_loop(0, 8, scale, 0)
        put_part(0, k, dot(wit[0], nt[g, 0]) + dot(wit[1], nt[g, 1]))

    def up_part(turn):
        k = offset(turn)
        g = xo(k)
        wait_sib(1, g)
        put_part(1, k, dot(wo[0], xt[1, g, 0]) + dot(wo[1], xt[1, g, 1]))

    def summed(arr):
        total = po[arr]
        for k in range(1, 4):
            other = pr.at[arr, xo(k)]
            remote(other, other, p_s.at[arr, k], p_r.at[arr, xo(k)], sibling).wait_recv()
            total = total + pr[arr, xo(k)].astype(F32)
        return total

    def hg_copy(arr, k):
        return remote(hg.at[arr, q], hg.at[arr, q], hg_s.at[arr, k], hg_r.at[arr, q], dev(h, xo(k), z, yl, c))

    def last_h():
        preact = summed(0)
        pre[...] = preact
        cumul, _ = gelu_parts(preact)
        hg[0, q] = (preact * cumul).astype(BF16)
        for k in (1, 3, 2):
            hg_copy(0, k).start()

    def sm_copy(stage):
        dst, to = ((smc, sibling), (smy, ypart))[stage]
        return remote(smo.at[stage], dst, sm_s.at[stage], sm_r.at[stage], to)

    def smz_copy(k):
        return remote(smo.at[2], smz.at[z], smz_s.at[k], smz_r.at[z], dev(h, q, zo(k), yl, c))

    def last_g():
        grad_hidden = summed(1)
        preact = pre[...]
        cumul, dense = gelu_parts(preact)
        grad = (grad_hidden * (cumul + preact * dense)).astype(BF16)
        hg[1, q] = grad
        for k in (1, 3, 2):
            hg_copy(1, k).start()
        by_gain = split_rows(jnp.sum(srow[...], axis=0, keepdims=True))
        smo[0, 0] = jnp.broadcast_to(jnp.sum(dot(by_gain, grad), axis=0, keepdims=True), (8, TG))
        inner = jnp.sum(grad.astype(F32) * preact, axis=0, keepdims=True)
        smo[0, 1] = jnp.broadcast_to(inner, (8, TG))
        sm_copy(0).start()

    def finish_h(slot):
        pl.when(odd == slot)(last_h)

    def finish_g(slot):
        pl.when(odd == slot)(last_g)

    def small_1():
        sm_copy(0).wait_recv()
        smo[1] = smo[0] + smc[...]
        sm_copy(1).start()

    def small_2():
        sm_copy(1).wait_recv()
        smo[2] = smo[1] + smy[...]
        for k in range(1, 8):
            smz_copy(k).start()

    def b_copy(arr, g, b):
        return remote(bp.at[arr, g, b, 1 - c], br.at[arr, g, b], b_s.at[arr, g, b], b_r.at[arr, g, b], sibling)

    def back_part(arr, turn):
        k = offset(turn)
        g = xo(k)

        @pl.when(k > 0)
        def _():
            other = hg.at[arr, g]
            remote(other, other, hg_s.at[arr, k], hg_r.at[arr, g], sibling).wait_recv()
        act = hg[arr, g]
        for b in range(2):
            for y2 in range(2):
                w = wot[b, y2 * 384 : (y2 + 1) * 384, :] if arr == 0 else wi[q + 4 * b, pl.ds(y2 * 384, 384), :]
                part = dot(w, act).astype(BF16)
                bp[arr, g, b, 0, y2] = part[:W]
                bp[arr, g, b, 1, y2] = part[W:]
            b_copy(arr, g, b).start()

    def rs_flags(rb, g, y2):
        from_up = (rb <= 2) | ((rb == 3) & (y2 == 0))
        from_down = (rb == 0) | (rb >= 6) | ((rb == 5) & (y2 == 1))
        to_down = ((rb >= 1) & (rb <= 3)) | ((rb == 4) & (y2 == 0))
        to_up = (rb >= 5) | ((rb == 4) & (y2 == 1))
        sink = rb == 0
        local = sink & (g == q) & (y2 == yl)
        return from_up, from_down, to_up, to_down, sink, local

    def rs_copies(b, arr, g, y2):
        piece = bp.at[arr, g, b, c, y2]
        sent, got = rz_s.at[arr, g, b, y2], rz_r.at[arr, g, b, y2]
        c_down = remote(piece, rz.at[arr, g, b, y2, 0], sent, got.at[0], zminus)
        c_up = remote(piece, rz.at[arr, g, b, y2, 1], sent, got.at[1], zplus)
        c_fin = remote(piece, fin.at[arr, yl], fin_s.at[arr, g, y2], fin_r.at[arr, yl], dev(h, g, z, y2, c))
        return c_up, c_down, c_fin

    def ry_copy(arr, g, b):
        return remote(bp.at[arr, g, b, c, 1 - yl], ry.at[arr, g, b], ry_s.at[arr, g, b], ry_r.at[arr, g, b], ypart)

    def rs_step(s):
        for b in range(2):
            rb, dist = place(b)
            n = s - LAG * (4 - dist)
            early = n + RYLAG

            @pl.when((early >= 0) & (early < 2 * RS_ITEMS))
            def _():
                arr, g, _, alone = item(early, 1)

                @pl.when(alone)
                def _():
                    b_copy(arr, g, b).wait_recv()
                    both = bp[arr, g, b, c, 1 - yl].astype(F32) + br[arr, g, b, 1 - yl].astype(F32)
                    bp[arr, g, b, c, 1 - yl] = both.astype(BF16)
                    ry_copy(arr, g, b).start()

            @pl.when((n >= 0) & (n < 2 * RS_ITEMS))
            def _():
                arr, g, y2, alone = item(n, 1)
                from_up, from_down, to_up, to_down, sink, local = rs_flags(rb, g, y2)
                c_up, c_down, c_fin = rs_copies(b, arr, g, y2)

                @pl.when((y2 == 0) & jnp.logical_not(alone))
                def _():
                    b_copy(arr, g, b).wait_recv()

                acc[...] = bp[arr, g, b, c, y2].astype(F32) + br[arr, g, b, y2].astype(F32)

                @pl.when(alone)
                def _():
                    ry_copy(arr, g, b).wait_recv()
                    acc[...] += ry[arr, g, b].astype(F32)

                @pl.when(from_up)
                def _():
                    c_down.wait_recv()
                    acc[...] += rz[arr, g, b, y2, 0].astype(F32)

                @pl.when(from_down)
                def _():
                    c_up.wait_recv()
                    acc[...] += rz[arr, g, b, y2, 1].astype(F32)

                bp[arr, g, b, c, y2] = acc[...].astype(BF16)
                pl.when(to_up)(c_up.start)
                pl.when(to_down)(c_down.start)
                pl.when(sink & jnp.logical_not(local))(c_fin.start)

                @pl.when(local)
                def _():
                    fin[arr, yl] = acc[...].astype(BF16)

    def gr_copy(i):
        return remote((gs, gso)[i].at[0], (gr, gro)[i].at[0], gr_s.at[i], gr_r.at[i], hpart)

    def grad_out_sent():
        for t in range(2):
            other = sum(dot_t(hg[0, g], xt[1, g, 1 - h, pl.ds(t * 384, 384), :]) for g in range(4))
            gso[0, :, t * 384 : (t + 1) * 384] = other.astype(BF16)
        gr_copy(1).start()

    def grad_out_own():
        for t in range(2):
            go_own[:, t * 384 : (t + 1) * 384] = sum(
                dot_t(hg[0, g], xt[1, g, h, pl.ds(t * 384, 384), :]) for g in range(4)
            )

    def grad_in_sent():
        for t in range(2):
            other = sum(dot_t(nt[g, 1 - h, pl.ds(t * 384, 384), :], hg[1, g]) for g in range(4))
            gs[0, t * 384 : (t + 1) * 384, :] = other.astype(BF16)
        gr_copy(0).start()

    def grad_in_own():
        for t in range(2):
            gi_own[t * 384 : (t + 1) * 384, :] = sum(
                dot_t(nt[g, h, pl.ds(t * 384, 384), :], hg[1, g]) for g in range(4)
            )

    turns = {}

    def at(step, run, *args):
        turns.setdefault(step, []).append(functools.partial(run, *args))

    at(1, merge_pair, 0)
    at(1, prep_wi, 0)
    at(2, prep_wi, 1)
    at(2, prep_gain)
    at(3, merge_pair, 1)
    for b in range(2):
        at(3 + b, prep_wit, b)
        at(6 + b, prep_wot, b)
        at(8 + b, prep_s, 4 * b, 4 * b + 4)
    at(5, merge_z)
    pair_a = AG_ITEMS // 2
    for i in range(4):
        at(FILL + pair_a * (i // 2 + 1) + EXTRA, norm_part, i)
        at(FILL + pair_a * (i // 2 + 3) + EXTRA, up_part, i)
        for arr in range(2):
            at(RS_START + RS_ITEMS * arr - 1 + BACK[i], back_part, arr, i)
    for slot in range(2):
        at(FILL + pair_a * (slot + 1) + LATE, finish_h, slot)
        at(FILL + pair_a * (slot + 3) + LATE, finish_g, slot)
    at(GRAD_OUT, grad_out_sent)
    at(RS_END - 4, grad_out_own)
    at(FILL + 2 * AG_ITEMS + LATE + 2, small_1)
    at(FILL + 2 * AG_ITEMS + LATE + 4, small_2)
    at(GRAD_IN, grad_in_sent)
    at(RS_END - 3, grad_in_own)

    def both(s, _):
        ag_step(s)
        rs_step(s - RS_START)
        return 0

    def first(s, _):
        ag_step(s)
        return 0

    def second(s, _):
        rs_step(s - RS_START)
        return 0

    marks = sorted(set(turns) | {0, RS_START, AG_END, RS_END})
    for lo, hi in zip(marks, marks[1:] + [RS_END]):
        for run in turns.get(lo, ()):
            run()
        if lo < hi:
            lax.fori_loop(lo, hi, first if lo < RS_START else both if lo < AG_END else second, 0)

    outs = ((gi_own, gi_ref), (go_own, go_ref), (out_own, out_ref), (gt_own, gt_ref))

    def put(i):
        return pltpu.make_async_copy(outs[i][0], outs[i][1], out_sem.at[i])

    gr_copy(1).wait_recv()
    go_own[...] += gro[0].astype(F32)
    put(1).start()
    gr_copy(0).wait_recv()
    gi_own[...] += gr[0].astype(F32)
    put(0).start()

    alone = (from_xs == 1) | (from_xs == 2) if RS_ALONE else from_xs < 0

    def fin_wait(arr):
        @pl.when(alone)
        def _():
            fin[arr, 1 - yl] = jnp.zeros((W, TG), BF16)

        for y2 in range(2):

            @pl.when(jnp.logical_not((xs == q) & (yl == y2)) & ((yl == y2) | jnp.logical_not(alone)))
            def _():
                piece = fin.at[arr, y2]
                remote(piece, piece, fin_s.at[arr, 0, y2], fin_r.at[arr, y2], sibling).wait_recv()

    fin_wait(0)
    out_own[...] = (x_ref[...].astype(F32) + (fin[0, 0].astype(F32) + fin[0, 1].astype(F32))).astype(BF16)

    sums = smo[2]
    for k in range(1, 8):
        remote(smz.at[zo(k)], smz.at[zo(k)], smz_s.at[k], smz_r.at[zo(k)], sibling).wait_recv()
        sums = sums + smz[zo(k)]
    mean, inv = stx[q, 0][None], stx[q, 1][None]
    unit = (x_ref[...].astype(F32).reshape(W // 8, 8, TG) - mean) * inv
    gain = gzcol[rows(yl, c), :]
    gain = jnp.concatenate([gain, gain], axis=1)
    fin_wait(1)
    scaled = ((fin[1, 0].astype(F32) + fin[1, 1].astype(F32)) * gain).reshape(W // 8, 8, TG)
    grad_ln = inv * (scaled - (sums[0] / D)[None] - unit * (sums[1] / D)[None])
    put(2).start()
    gt_own[...] = (u_ref[...].astype(F32) + grad_ln.reshape(W, TG)).astype(BF16)


    put(3).start()

    for arr in range(2):
        pl.when(xs != q)(origin(arr, 0).wait_send)
        pl.when(jnp.logical_not(own_only(from_xs)))(origin(arr, 1).wait_send)
        for k in range(1, 4):
            hg_copy(arr, k).wait_send()
            p_copy(arr, k).wait_send()
    for i in range(2):
        gr_copy(i).wait_send()
        sm_copy(i).wait_send()
    for k in range(1, 8):
        smz_copy(k).wait_send()

    def drain_ag(n, _):
        for b in range(2):
            rb, _ = place(b)
            up, down, _, alone, c_up, c_down, c_y, c_sib = ag_copies(b, rb, n)
            arr, g, _, _ = item(n, 0)
            pl.when(up)(c_up.wait_send)
            pl.when(down)(c_down.wait_send)
            c_sib.wait_send()

            @pl.when(alone)
            def _():
                c_y.wait_send()
                sib_copy(arr, g, b, 1 - yl, c).wait_send()

        return 0

    def drain_rs(n, _):
        for b in range(2):
            rb, _ = place(b)
            arr, g, y2, alone = item(n, 1)
            _, _, to_up, to_down, sink, local = rs_flags(rb, g, y2)
            c_up, c_down, c_fin = rs_copies(b, arr, g, y2)
            pl.when(to_up)(c_up.wait_send)
            pl.when(to_down)(c_down.wait_send)
            pl.when(sink & jnp.logical_not(local))(c_fin.wait_send)
            pl.when(alone)(ry_copy(arr, g, b).wait_send)
            pl.when((y2 == 0) | alone)(b_copy(arr, g, b).wait_send)
        return 0

    lax.fori_loop(0, 2 * AG_ITEMS, drain_ag, 0)
    lax.fori_loop(0, 2 * RS_ITEMS, drain_rs, 0)

    for k in range(1, 8):
        stz_copy(k).wait_send()
    for k in range(1, 4):
        stx_copy(k).wait_send()
    for i in range(2):
        st_copy(i).wait_send()
    for i in range(4):
        put(i).wait()


def finish(*refs):
    sources, results, held, sems = refs[:4], refs[4:8], refs[8:12], refs[12]
    jobs = []
    for i in range(4):
        size = sources[i].shape[0]
        step = size // (4 if i > 1 else 1)
        for t in range(0, size, step):
            part, k = pl.ds(t, step), len(jobs)
            jobs.append(
                (
                    pltpu.make_async_copy(sources[i].at[part], held[i].at[part], sems.at[0, k]),
                    pltpu.make_async_copy(held[i].at[part], results[i].at[part], sems.at[1, k]),
                )
            )
    for first, _ in jobs:
        first.start()
    for first, second in jobs:
        first.wait()
        second.start()
    for _, second in jobs:
        second.wait()


def body(tokens, upstream, norm_gain, w_in, w_out):
    sem = pltpu.SemaphoreType.DMA
    vmem = pl.BlockSpec(memory_space=pltpu.VMEM)
    hbm = pl.BlockSpec(memory_space=pl.ANY)
    scratch = [
        pltpu.VMEM((2, 4, 2, BLK, TG), BF16),
        pltpu.VMEM((4, 2, BLK, TG), BF16),
        pltpu.VMEM((8, BLK, FB), BF16),
        pltpu.VMEM((2, FB, BLK), BF16),
        pltpu.VMEM((2, FB, BLK), BF16),
        pltpu.VMEM((2, BLK, FB), BF16),
        pltpu.VMEM((2, BLK, 128), F32),
        pltpu.VMEM((BLK, 128), F32),
        pltpu.VMEM((16, FB), F32),
        pltpu.VMEM((8, BLK), F32),
        pltpu.VMEM((3, 2, 8, TG), F32),
        pltpu.VMEM((2, 2, 8, TG), F32),
        pltpu.VMEM((8, 2, 8, TG), F32),
        pltpu.VMEM((4, 2, 8, TG), F32),
        pltpu.VMEM((2, 4, FB, TG), BF16),
        pltpu.VMEM((2, 4, FB, TG), BF16),
        pltpu.VMEM((2, FB, TG), F32),
        pltpu.VMEM((FB, TG), F32),
        pltpu.VMEM((2, 4, FB, TG), BF16),
        pltpu.VMEM((2, 4, 2, 2, 2, W, TG), BF16),
        pltpu.VMEM((2, 4, 2, 2, W, TG), BF16),
        pltpu.VMEM((2, 4, 2, 2, 2, W, TG), BF16),
        pltpu.VMEM((2, 4, 2, W, TG), BF16),
        pltpu.VMEM((W, TG), F32),
        pltpu.VMEM((2, 2, W, TG), BF16),
        pltpu.VMEM((3, 2, 8, TG), F32),
        pltpu.VMEM((2, 8, TG), F32),
        pltpu.VMEM((2, 8, TG), F32),
        pltpu.VMEM((8, 2, 8, TG), F32),
        pltpu.VMEM((1, BLK, FB), BF16),
        pltpu.VMEM((1, BLK, FB), BF16),
        pltpu.VMEM((1, FB, BLK), BF16),
        pltpu.VMEM((1, FB, BLK), BF16),
        pltpu.VMEM((BLK, FB), F32),
        pltpu.VMEM((FB, BLK), F32),
        pltpu.VMEM((W, TG), BF16),
        pltpu.VMEM((W, TG), BF16),
        sem((10,)),
        sem((2, 2)),
        sem((2, 4, 2, 2)),
        sem((2, 4, 2, 2, 2)),
        sem((2, 4, 2)),
        sem((2, 4, 2, 2)),
        sem((2, 4, 2, 2)),
        sem((2,)),
        sem((2,)),
        sem((8,)),
        sem((8,)),
        sem((4,)),
        sem((4,)),
        sem((2, 4)),
        sem((2, 4)),
        sem((2, 4)),
        sem((2, 4)),
        sem((2, 4, 2)),
        sem((2, 4, 2)),
        sem((2, 4, 2, 2)),
        sem((2, 4, 2, 2, 2)),
        sem((2, 4, 2)),
        sem((2, 4, 2)),
        sem((2, 4, 2)),
        sem((2, 2)),
        sem((2,)),
        sem((2,)),
        sem((8,)),
        sem((8,)),
        sem((2,)),
        sem((2,)),
        sem((4,)),
    ]
    shapes = (
        jax.ShapeDtypeStruct((W, TG), BF16),
        jax.ShapeDtypeStruct((W, TG), BF16),
        jax.ShapeDtypeStruct((BLK, FB), F32),
        jax.ShapeDtypeStruct((FB, BLK), F32),
    )
    results = pl.pallas_call(
        kernel,
        out_shape=shapes,
        in_specs=[vmem, vmem, vmem, hbm, hbm],
        out_specs=(hbm,) * 4,
        scratch_shapes=scratch,
        compiler_params=pltpu.CompilerParams(
            collective_id=1, has_side_effects=True, vmem_limit_bytes=58 << 20
        ),
        name="block",
    )(tokens.T, upstream.T, norm_gain, w_in, w_out)
    out_t, grad_t, grad_in, grad_out = pl.pallas_call(
        finish,
        out_shape=shapes,
        in_specs=[hbm] * 4,
        out_specs=(hbm,) * 4,
        scratch_shapes=[pltpu.VMEM(a.shape, a.dtype) for a in shapes] + [sem((2, 10))],
        name="finish",
    )(*results)
    return out_t.T, grad_t.T, grad_in, grad_out


def solution(mesh):
    return jax.shard_map(
        body,
        mesh=mesh,
        in_specs=(P("dp", "mp"), P("dp", "mp"), P(), P(None, "mp"), P("mp", None)),
        out_specs=(P("dp", "mp"), P("dp", "mp"), P("dp", "mp"), P("mp", "dp")),
        check_vma=False,
    )
```

```python
import functools

import jax
import jax.numpy as jnp
from jax import lax
from jax.experimental import pallas as pl
from jax.experimental.pallas import tpu as pltpu
from jax.sharding import PartitionSpec as P

MESH = pl.DeviceIdType.MESH
F32, BF16 = jnp.float32, jnp.bfloat16
D = 6144
BLK = 768
W = 192
TG = 256
FB = 384
ORDER = ((0, 2, 1, 3), (0, 2, 3, 1))
HG_ORDER = (1, 3, 2)
PLAN5 = ((0, 2), (1, 2), (2, 2), (3, 0), (3, 1))
PLAN6 = ((0, 2), (1, 0), (1, 1), (2, 2), (3, 0), (3, 1))
PLAN6R = ((0, 0), (0, 1), (1, 2), (2, 0), (2, 1), (3, 2))
PLAN7R = ((0, 0), (0, 1), (1, 2), (2, 0), (2, 1), (3, 0), (3, 1))
PLAN8 = tuple((t, y) for t in range(4) for y in range(2))
AG_PLAN = PLAN5
RS_PLAN = PLAN8
AG_ITEMS = len(AG_PLAN)
RS_ITEMS = len(RS_PLAN)
LAG = 2
YLAG = 2
RYLAG = 2
FILL = 4 * LAG
AG_END = 2 * AG_ITEMS + FILL
RS_START = 21
RS_END = RS_START + 2 * RS_ITEMS + FILL
LATE = 5
SLOTS = 0
ORIGIN_U = 1
BACK = ((0, 2, 4, 6), (0, 2, 4, 5))
GRAD_OUT = RS_START + 6
GRAD_IN = RS_START + 12
OWN = 4


def alone_turns(plan):
    return tuple(t for t, y in plan if y == 2)


def done(arr, turn):
    last = max(i + (YLAG if y == 2 else 0) for i, (t, y) in enumerate(AG_PLAN) if t == turn)
    return FILL + arr * AG_ITEMS + last + 1


def choose(table, i):
    value = jnp.int32(table[-1])
    for k in range(len(table) - 1):
        value = jnp.where(i == k, jnp.int32(table[k]), value)
    return value


def gelu_parts(v):
    cumul = 0.5 * (1.0 + lax.erf(v * 0.7071067811865476))
    dense = jnp.exp(-0.5 * v * v) * 0.3989422804014327
    return cumul, dense


def split_rows(row):
    n = row.shape[1]
    hi = row.astype(BF16).astype(F32)
    mid = (row - hi).astype(BF16).astype(F32)
    low = row - hi - mid
    index = lax.broadcasted_iota(jnp.int32, (16, n), 0)
    spread = [jnp.broadcast_to(v, (16, n)) for v in (hi, mid, low)]
    zero = jnp.zeros((16, n), F32)
    out = jnp.where(
        index == 0, spread[0], jnp.where(index == 1, spread[1], jnp.where(index == 2, spread[2], zero))
    )
    return out.astype(BF16)


def column(row):
    return jnp.broadcast_to(row, (128, row.shape[1])).T


def dot(a, b):
    return jnp.dot(a, b, preferred_element_type=F32)


def dot_t(a, b):
    return lax.dot_general(a, b, (((1,), (1,)), ((), ())), preferred_element_type=F32)


def kernel(
    x_ref, u_ref, gain_ref, w_in_ref, w_out_ref,
    out_ref, gt_ref, gi_ref, go_ref,
    xt, nt, wi, wit, wo, wot, gcol, gzcol, srow,
    gain8, st, stm, stz, stx, ps, pr, po, pre, hg,
    bp, br, rz, ry, acc, fin, smo, smc, smy, smz, gs, gr, gso, gro, gi_own, go_own, out_own, gt_own,
    loc_sem, org_s, ag_r, ag_z, ag_y, sib_s, sib_r, st_s, st_r, stz_s, stz_r, stx_s, stx_r, p_s, p_r, hg_s, hg_r,
    b_s, b_r, rz_s, rz_r, ry_s, ry_r, fin_s, fin_r, sm_s, sm_r, smz_s, smz_r, gr_s, gr_r, out_sem,
):
    dp, mp = lax.axis_index("dp"), lax.axis_index("mp")
    h, q = lax.div(dp, 4), lax.rem(dp, 4)
    z, yl, c = lax.div(mp, 4), lax.rem(lax.div(mp, 2), 2), lax.rem(mp, 2)

    def dev(h_, x_, z_, y_, c_):
        return (h_ * 4 + x_, z_ * 4 + y_ * 2 + c_)

    def xo(k):
        return lax.rem(q + k, 4)

    def zo(k):
        return lax.rem(z + k, 8)

    sibling = dev(h, q, z, yl, 1 - c)
    ypart = dev(h, q, z, 1 - yl, c)
    hpart = dev(1 - h, q, z, yl, c)
    zplus, zminus = dev(h, q, zo(1), yl, c), dev(h, q, zo(7), yl, c)

    def remote(src, dst, ss, rs, to):
        return pltpu.make_async_remote_copy(
            src_ref=src, dst_ref=dst, send_sem=ss, recv_sem=rs, device_id=to, device_id_type=MESH
        )

    def wi_copy(k):
        return pltpu.make_async_copy(w_in_ref.at[pl.ds(k * BLK, BLK)], wi.at[k], loc_sem.at[k])

    def wo_copy(b):
        start = pl.multiple_of((q + 4 * b) * BLK, BLK)
        return pltpu.make_async_copy(w_out_ref.at[:, pl.ds(start, BLK)], wo.at[b], loc_sem.at[8 + b])

    for k in range(8):
        wi_copy(k).start()
    for b in range(2):
        wo_copy(b).start()

    partners = [sibling, ypart, hpart]
    partners += [dev(h, q, zo(k), yl, c) for k in range(1, 8)]
    partners += [dev(h, xo(k), z, y_, c) for k in range(1, 4) for y_ in (yl, 1 - yl)]
    barrier = pltpu.get_barrier_semaphore()
    for p in partners:
        pl.semaphore_signal(barrier, inc=1, device_id=p, device_id_type=MESH)
    pl.semaphore_wait(barrier, len(partners))

    def rows(y2, cc):
        return pl.ds(pl.multiple_of(y2 * 384 + cc * W, 64), W)

    xs = lax.rem(z, 4)
    zb = lax.div(z, 4)
    mine = (x_ref, u_ref)

    def own_only(plan, k, par):
        out = k < 0
        for t in alone_turns(plan):
            out = out | (k == jnp.where(par == 1, ORDER[1][t], ORDER[0][t]))
        return out

    from_xs = lax.rem(q - xs + 4, 4)

    def origin(arr, other):
        to = dev(h, xs, z, 1 - yl if other else yl, c)
        return remote(
            mine[arr], xt.at[arr, q, zb, rows(yl, c)], org_s.at[arr, other], ag_r.at[arr, q, zb, yl], to
        )

    crosses = jnp.logical_not(own_only(AG_PLAN, from_xs, lax.rem(xs, 2)))

    def origin_sends(arr):
        pl.when(xs != q)(origin(arr, 0).start)
        pl.when(crosses)(origin(arr, 1).start)

    origin_sends(0)

    @pl.when(xs == q)
    def _():
        for arr in range(2):
            xt[arr, q, zb, rows(yl, c), :] = mine[arr][...]

    def st_copy(stage):
        return remote(st.at[stage], stm.at[stage], st_s.at[stage], st_r.at[stage], (sibling, ypart)[stage])

    def stz_copy(k):
        return remote(st.at[2], stz.at[z], stz_s.at[k], stz_r.at[z], dev(h, q, zo(k), yl, c))

    def stx_copy(k):
        return remote(stx.at[q], stx.at[q], stx_s.at[k], stx_r.at[q], dev(h, xo(k), z, yl, c))

    def own_stats():
        piece = x_ref[...].astype(F32).reshape(W // 8, 8, TG)
        total = jnp.sum(jnp.sum(piece, axis=0), axis=0, keepdims=True)
        mean = jnp.broadcast_to(total * (1.0 / W), (8, TG))
        d = piece - mean[None]
        st[0, 0] = mean
        spread = jnp.sum(jnp.sum(d * d, axis=0), axis=0, keepdims=True)
        st[0, 1] = jnp.broadcast_to(spread, (8, TG))
        st_copy(0).start()

    def merge(parts, count):
        mean = sum(p[0] for p in parts) * (1.0 / len(parts))
        spread = sum(p[1] for p in parts)
        for p in parts:
            spread = spread + (p[0] - mean) * (p[0] - mean) * float(count)
        return mean, spread

    def merge_pair(stage):
        st_copy(stage).wait_recv()
        parts = [(st[stage, 0], st[stage, 1]), (stm[stage, 0], stm[stage, 1])]
        st[stage + 1, 0], st[stage + 1, 1] = merge(parts, W * (stage + 1))
        if stage == 0:
            st_copy(1).start()
        else:
            for k in range(1, 8):
                stz_copy(k).start()

    def merge_z():
        parts = [(st[2, 0], st[2, 1])]
        for k in range(1, 8):
            other = stz.at[zo(k)]
            remote(other, other, stz_s.at[k], stz_r.at[zo(k)], sibling).wait_recv()
            parts.append((stz[zo(k), 0], stz[zo(k), 1]))
        mean, spread = merge(parts, 4 * W)
        stx[q, 0] = mean
        stx[q, 1] = lax.rsqrt(spread / D + 1e-06)
        for k in range(1, 4):
            stx_copy(k).start()

    own_stats()

    odd = lax.rem(q, 2)

    def offset(turn):
        off = [jnp.where(odd == 1, ORDER[1][i], ORDER[0][i]) for i in range(4)]
        if isinstance(turn, int):
            return off[turn]
        return jnp.where(turn < 2, jnp.where(turn == 0, off[0], off[1]), jnp.where(turn == 2, off[2], off[3]))

    def item(n, plan):
        arr, m = lax.div(n, len(plan)), lax.rem(n, len(plan))
        half = choose([y for _, y in plan], m)
        alone = half == 2
        k = offset(choose([t for t, _ in plan], m))
        return arr, xo(k), jnp.where(alone, yl, half), alone

    def place(b):
        rb = lax.rem(z - q + 8 - 4 * b, 8)
        return rb, jnp.minimum(rb, 8 - rb)

    def sib_copy(arr, g, b, y2, cc):
        piece = xt.at[arr, g, b, rows(y2, cc)]
        return remote(piece, piece, sib_s.at[arr, g, b, y2], sib_r.at[arr, g, b, y2], sibling)

    def ag_copies(b, rb, n):
        arr, g, y2, alone = item(n, AG_PLAN)
        piece = xt.at[arr, g, b, rows(y2, c)]
        recv = ag_r.at[arr, g, b, y2]
        up = (rb <= 2) | ((rb == 3) & (y2 == 0))
        down = (rb == 0) | (rb >= 6) | ((rb == 5) & (y2 == 1))
        local = (rb == 0) & (g == q) & (y2 == yl)
        c_up = remote(piece, piece, ag_z.at[arr, g, b, y2, 0], recv, zplus)
        c_down = remote(piece, piece, ag_z.at[arr, g, b, y2, 1], recv, zminus)
        c_y = remote(piece, piece, ag_y.at[arr, g, b], recv, ypart)
        return up, down, local, alone, c_up, c_down, c_y, sib_copy(arr, g, b, y2, c)

    def ag_step(s):
        for b in range(2):
            rb, dist = place(b)
            n = s - LAG * dist

            @pl.when((n >= 0) & (n < 2 * AG_ITEMS))
            def _():
                up, down, local, alone, c_up, c_down, c_y, c_sib = ag_copies(b, rb, n)

                @pl.when(jnp.logical_not(local))
                def _():
                    c_up.wait_recv()

                c_sib.start()
                pl.when(up)(c_up.start)
                pl.when(down)(c_down.start)
                pl.when(alone)(c_y.start)

        for b in range(2):
            _, dist = place(b)
            late = s - LAG * dist - YLAG

            @pl.when((late >= 0) & (late < 2 * AG_ITEMS))
            def _():
                arr, g, _, alone = item(late, AG_PLAN)

                @pl.when(alone)
                def _():
                    c_sib = sib_copy(arr, g, b, 1 - yl, c)
                    piece = xt.at[arr, g, b, rows(1 - yl, c)]
                    remote(piece, piece, ag_y.at[arr, g, b], ag_r.at[arr, g, b, 1 - yl], ypart).wait_recv()
                    c_sib.start()

    def prep_wi(b):
        for k in range(4 * b, 4 * b + 4):
            wi_copy(k).wait()

    def prep_s(lo, hi):
        for k in range(lo, hi):
            term = dot(split_rows(gain8[k : k + 1, :]), wi[k])
            if k == 0:
                srow[...] = term
            else:
                srow[...] += term

    def prep_wit(b):
        for t in range(2):
            part = wi[q + 4 * b, pl.ds(t * 384, 384), :]
            wit[b, :, t * 384 : (t + 1) * 384] = part.T

    def prep_wot(b):
        wo_copy(b).wait()
        for t in range(2):
            wot[b, t * 384 : (t + 1) * 384, :] = wo[b, :, t * 384 : (t + 1) * 384].T

    def prep_gain():
        for k in range(8):
            gain8[k : k + 1, :] = gain_ref[k * BLK : (k + 1) * BLK].reshape(1, BLK)
        for b in range(2):
            gcol[b] = column(gain8[pl.ds(q + 4 * b, 1), :])
        gzcol[...] = column(gain8[pl.ds(z, 1), :])

    def wait_sib(arr, g):
        for b in range(2):
            for y2 in range(2):
                sib_copy(arr, g, b, y2, 1 - c).wait_recv()

    def p_copy(arr, k):
        return remote(ps.at[arr, xo(k)], pr.at[arr, q], p_s.at[arr, k], p_r.at[arr, q], dev(h, xo(k), z, yl, c))

    def put_part(arr, k, part):
        @pl.when(k == 0)
        def _():
            po[arr] = part

        @pl.when(k > 0)
        def _():
            ps[arr, xo(k)] = part.astype(BF16)
            p_copy(arr, k).start()

    def norm_part(turn):
        k = offset(turn)
        g = xo(k)
        wait_sib(0, g)

        @pl.when(k > 0)
        def _():
            other = stx.at[g]
            remote(other, other, stx_s.at[k], stx_r.at[g], sibling).wait_recv()

        mean, inv = stx[g, 0], stx[g, 1]

        def scale(i, _):
            b = lax.div(i, 4)
            r = pl.ds(pl.multiple_of(lax.rem(i, 4) * W, 64), W)
            piece = xt[0, g, b, r, :].astype(F32).reshape(W // 8, 8, TG)
            unit = ((piece - mean[None]) * inv[None]).reshape(W, TG)
            gain = gcol[b, r, :]
            nt[g, b, r, :] = (unit * jnp.concatenate([gain, gain], axis=1)).astype(BF16)
            return 0

        lax.fori_loop(0, 8, scale, 0)
        put_part(0, k, dot(wit[0], nt[g, 0]) + dot(wit[1], nt[g, 1]))

    def up_part(turn):
        k = offset(turn)
        g = xo(k)
        wait_sib(1, g)
        put_part(1, k, dot(wo[0], xt[1, g, 0]) + dot(wo[1], xt[1, g, 1]))

    def summed(arr):
        total = po[arr]
        for k in range(1, 4):
            other = pr.at[arr, xo(k)]
            remote(other, other, p_s.at[arr, k], p_r.at[arr, xo(k)], sibling).wait_recv()
            total = total + pr[arr, xo(k)].astype(F32)
        return total

    def hg_copy(arr, k):
        return remote(hg.at[arr, q], hg.at[arr, q], hg_s.at[arr, k], hg_r.at[arr, q], dev(h, xo(k), z, yl, c))

    def last_h():
        preact = summed(0)
        pre[...] = preact
        cumul, _ = gelu_parts(preact)
        hg[0, q] = (preact * cumul).astype(BF16)
        for k in HG_ORDER:
            hg_copy(0, k).start()

    def sm_copy(stage):
        dst, to = ((smc, sibling), (smy, ypart))[stage]
        return remote(smo.at[stage], dst, sm_s.at[stage], sm_r.at[stage], to)

    def smz_copy(k):
        return remote(smo.at[2], smz.at[z], smz_s.at[k], smz_r.at[z], dev(h, q, zo(k), yl, c))

    def last_g():
        grad_hidden = summed(1)
        preact = pre[...]
        cumul, dense = gelu_parts(preact)
        grad = (grad_hidden * (cumul + preact * dense)).astype(BF16)
        hg[1, q] = grad
        for k in HG_ORDER:
            hg_copy(1, k).start()
        by_gain = split_rows(jnp.sum(srow[...], axis=0, keepdims=True))
        smo[0, 0] = jnp.broadcast_to(jnp.sum(dot(by_gain, grad), axis=0, keepdims=True), (8, TG))
        inner = jnp.sum(grad.astype(F32) * preact, axis=0, keepdims=True)
        smo[0, 1] = jnp.broadcast_to(inner, (8, TG))
        sm_copy(0).start()

    def finish_h(slot):
        pl.when(odd == slot)(last_h)

    def finish_g(slot):
        pl.when(odd == slot)(last_g)

    def small_1():
        sm_copy(0).wait_recv()
        smo[1] = smo[0] + smc[...]
        sm_copy(1).start()

    def small_2():
        sm_copy(1).wait_recv()
        smo[2] = smo[1] + smy[...]
        for k in range(1, 8):
            smz_copy(k).start()

    def b_copy(arr, g, b):
        return remote(bp.at[arr, g, b, 1 - c], br.at[arr, g, b], b_s.at[arr, g, b], b_r.at[arr, g, b], sibling)

    def back_part(arr, turn):
        k = offset(turn)
        g = xo(k)

        @pl.when(k > 0)
        def _():
            other = hg.at[arr, g]
            remote(other, other, hg_s.at[arr, k], hg_r.at[arr, g], sibling).wait_recv()
        act = hg[arr, g]
        for b in range(2):
            for y2 in range(2):
                w = wot[b, y2 * 384 : (y2 + 1) * 384, :] if arr == 0 else wi[q + 4 * b, pl.ds(y2 * 384, 384), :]
                part = dot(w, act).astype(BF16)
                bp[arr, g, b, 0, y2] = part[:W]
                bp[arr, g, b, 1, y2] = part[W:]
            b_copy(arr, g, b).start()

    def rs_flags(rb, g, y2):
        from_up = (rb <= 2) | ((rb == 3) & (y2 == 0))
        from_down = (rb == 0) | (rb >= 6) | ((rb == 5) & (y2 == 1))
        to_down = ((rb >= 1) & (rb <= 3)) | ((rb == 4) & (y2 == 0))
        to_up = (rb >= 5) | ((rb == 4) & (y2 == 1))
        sink = rb == 0
        local = sink & (g == q) & (y2 == yl)
        return from_up, from_down, to_up, to_down, sink, local

    def rs_copies(b, arr, g, y2):
        piece = bp.at[arr, g, b, c, y2]
        sent, got = rz_s.at[arr, g, b, y2], rz_r.at[arr, g, b, y2]
        c_down = remote(piece, rz.at[arr, g, b, y2, 0], sent, got.at[0], zminus)
        c_up = remote(piece, rz.at[arr, g, b, y2, 1], sent, got.at[1], zplus)
        c_fin = remote(piece, fin.at[arr, yl], fin_s.at[arr, g, y2], fin_r.at[arr, yl], dev(h, g, z, y2, c))
        return c_up, c_down, c_fin

    def ry_copy(arr, g, b):
        return remote(bp.at[arr, g, b, c, 1 - yl], ry.at[arr, g, b], ry_s.at[arr, g, b], ry_r.at[arr, g, b], ypart)

    def rs_step(s):
        for b in range(2):
            rb, dist = place(b)
            n = s - LAG * (4 - dist)
            early = n + RYLAG

            @pl.when((early >= 0) & (early < 2 * RS_ITEMS))
            def _():
                arr, g, _, alone = item(early, RS_PLAN)

                @pl.when(alone)
                def _():
                    b_copy(arr, g, b).wait_recv()
                    both = bp[arr, g, b, c, 1 - yl].astype(F32) + br[arr, g, b, 1 - yl].astype(F32)
                    bp[arr, g, b, c, 1 - yl] = both.astype(BF16)
                    ry_copy(arr, g, b).start()

            @pl.when((n >= 0) & (n < 2 * RS_ITEMS))
            def _():
                arr, g, y2, alone = item(n, RS_PLAN)
                from_up, from_down, to_up, to_down, sink, local = rs_flags(rb, g, y2)
                c_up, c_down, c_fin = rs_copies(b, arr, g, y2)

                @pl.when((y2 == 0) & jnp.logical_not(alone))
                def _():
                    b_copy(arr, g, b).wait_recv()

                acc[...] = bp[arr, g, b, c, y2].astype(F32) + br[arr, g, b, y2].astype(F32)

                @pl.when(alone)
                def _():
                    ry_copy(arr, g, b).wait_recv()
                    acc[...] += ry[arr, g, b].astype(F32)

                @pl.when(from_up)
                def _():
                    c_down.wait_recv()
                    acc[...] += rz[arr, g, b, y2, 0].astype(F32)

                @pl.when(from_down)
                def _():
                    c_up.wait_recv()
                    acc[...] += rz[arr, g, b, y2, 1].astype(F32)

                bp[arr, g, b, c, y2] = acc[...].astype(BF16)
                pl.when(to_up)(c_up.start)
                pl.when(to_down)(c_down.start)
                pl.when(sink & jnp.logical_not(local))(c_fin.start)

                @pl.when(local)
                def _():
                    fin[arr, yl] = acc[...].astype(BF16)

    def gr_copy(i):
        return remote((gs, gso)[i].at[0], (gr, gro)[i].at[0], gr_s.at[i], gr_r.at[i], hpart)

    def grad_out_sent():
        for t in range(2):
            other = sum(dot_t(hg[0, g], xt[1, g, 1 - h, pl.ds(t * 384, 384), :]) for g in range(4))
            gso[0, :, t * 384 : (t + 1) * 384] = other.astype(BF16)
        gr_copy(1).start()

    def grad_out_own():
        for t in range(2):
            go_own[:, t * 384 : (t + 1) * 384] = sum(
                dot_t(hg[0, g], xt[1, g, h, pl.ds(t * 384, 384), :]) for g in range(4)
            )

    def grad_in_sent():
        for t in range(2):
            other = sum(dot_t(nt[g, 1 - h, pl.ds(t * 384, 384), :], hg[1, g]) for g in range(4))
            gs[0, t * 384 : (t + 1) * 384, :] = other.astype(BF16)
        gr_copy(0).start()

    def grad_in_own():
        for t in range(2):
            gi_own[t * 384 : (t + 1) * 384, :] = sum(
                dot_t(nt[g, h, pl.ds(t * 384, 384), :], hg[1, g]) for g in range(4)
            )

    turns = {}

    def at(step, run, *args):
        turns.setdefault(step, []).append(functools.partial(run, *args))

    at(1, merge_pair, 0)
    at(1, prep_wi, 0)
    at(2, prep_wi, 1)
    at(2, prep_gain)
    at(3, merge_pair, 1)
    for b in range(2):
        at(3 + b, prep_wit, b)
        at(6 + b, prep_wot, b)
        at(8 + b, prep_s, 4 * b, 4 * b + 4)
    at(5, merge_z)
    at(ORIGIN_U, origin_sends, 1)
    for i in range(4):
        at(done(0, i), norm_part, i)
        at(done(1, i), up_part, i)
        for arr in range(2):
            at(RS_START + RS_ITEMS * arr - 1 + BACK[arr][i], back_part, arr, i)
    for slot in range(2):
        last = (2 * slot, 2 * slot + 1) if SLOTS else range(4)
        at(max(done(0, i) for i in last) + LATE, finish_h, slot)
        at(max(done(1, i) for i in last) + LATE, finish_g, slot)
    at(GRAD_OUT, grad_out_sent)
    at(RS_END - OWN, grad_out_own)
    at(max(done(1, 2), done(1, 3)) + LATE + 2, small_1)
    at(max(done(1, 2), done(1, 3)) + LATE + 4, small_2)
    at(GRAD_IN, grad_in_sent)
    at(RS_END - OWN + 1, grad_in_own)

    def both(s, _):
        ag_step(s)
        rs_step(s - RS_START)
        return 0

    def first(s, _):
        ag_step(s)
        return 0

    def second(s, _):
        rs_step(s - RS_START)
        return 0

    marks = sorted(set(turns) | {0, RS_START - 2, AG_END, RS_END})
    for lo, hi in zip(marks, marks[1:] + [RS_END]):
        for run in turns.get(lo, ()):
            run()
        if lo < hi:
            lax.fori_loop(lo, hi, first if lo < RS_START - 2 else both if lo < AG_END else second, 0)

    outs = ((gi_own, gi_ref), (go_own, go_ref), (out_own, out_ref), (gt_own, gt_ref))

    def put(i):
        return pltpu.make_async_copy(outs[i][0], outs[i][1], out_sem.at[i])

    gr_copy(1).wait_recv()
    go_own[...] += gro[0].astype(F32)
    put(1).start()
    gr_copy(0).wait_recv()
    gi_own[...] += gr[0].astype(F32)
    put(0).start()

    alone = own_only(RS_PLAN, from_xs, lax.rem(xs, 2))

    def fin_wait(arr):
        @pl.when(alone)
        def _():
            fin[arr, 1 - yl] = jnp.zeros((W, TG), BF16)

        for y2 in range(2):

            @pl.when(jnp.logical_not((xs == q) & (yl == y2)) & ((yl == y2) | jnp.logical_not(alone)))
            def _():
                piece = fin.at[arr, y2]
                remote(piece, piece, fin_s.at[arr, 0, y2], fin_r.at[arr, y2], sibling).wait_recv()

    fin_wait(0)
    out_own[...] = (x_ref[...].astype(F32) + (fin[0, 0].astype(F32) + fin[0, 1].astype(F32))).astype(BF16)

    sums = smo[2]
    for k in range(1, 8):
        remote(smz.at[zo(k)], smz.at[zo(k)], smz_s.at[k], smz_r.at[zo(k)], sibling).wait_recv()
        sums = sums + smz[zo(k)]
    mean, inv = stx[q, 0][None], stx[q, 1][None]
    unit = (x_ref[...].astype(F32).reshape(W // 8, 8, TG) - mean) * inv
    gain = gzcol[rows(yl, c), :]
    gain = jnp.concatenate([gain, gain], axis=1)
    fin_wait(1)
    scaled = ((fin[1, 0].astype(F32) + fin[1, 1].astype(F32)) * gain).reshape(W // 8, 8, TG)
    grad_ln = inv * (scaled - (sums[0] / D)[None] - unit * (sums[1] / D)[None])
    put(2).start()
    gt_own[...] = (u_ref[...].astype(F32) + grad_ln.reshape(W, TG)).astype(BF16)


    put(3).start()

    for arr in range(2):
        pl.when(xs != q)(origin(arr, 0).wait_send)
        pl.when(crosses)(origin(arr, 1).wait_send)
        for k in range(1, 4):
            hg_copy(arr, k).wait_send()
            p_copy(arr, k).wait_send()
    for i in range(2):
        gr_copy(i).wait_send()
        sm_copy(i).wait_send()
    for k in range(1, 8):
        smz_copy(k).wait_send()

    def drain_ag(n, _):
        for b in range(2):
            rb, _ = place(b)
            up, down, _, alone, c_up, c_down, c_y, c_sib = ag_copies(b, rb, n)
            arr, g, _, _ = item(n, AG_PLAN)
            pl.when(up)(c_up.wait_send)
            pl.when(down)(c_down.wait_send)
            c_sib.wait_send()

            @pl.when(alone)
            def _():
                c_y.wait_send()
                sib_copy(arr, g, b, 1 - yl, c).wait_send()

        return 0

    def drain_rs(n, _):
        for b in range(2):
            rb, _ = place(b)
            arr, g, y2, alone = item(n, RS_PLAN)
            _, _, to_up, to_down, sink, local = rs_flags(rb, g, y2)
            c_up, c_down, c_fin = rs_copies(b, arr, g, y2)
            pl.when(to_up)(c_up.wait_send)
            pl.when(to_down)(c_down.wait_send)
            pl.when(sink & jnp.logical_not(local))(c_fin.wait_send)
            pl.when(alone)(ry_copy(arr, g, b).wait_send)
            pl.when((y2 == 0) | alone)(b_copy(arr, g, b).wait_send)
        return 0

    lax.fori_loop(0, 2 * AG_ITEMS, drain_ag, 0)
    lax.fori_loop(0, 2 * RS_ITEMS, drain_rs, 0)

    for k in range(1, 8):
        stz_copy(k).wait_send()
    for k in range(1, 4):
        stx_copy(k).wait_send()
    for i in range(2):
        st_copy(i).wait_send()
    for i in range(4):
        put(i).wait()


def finish(*refs):
    sources, results, held, sems = refs[:4], refs[4:8], refs[8:12], refs[12]
    jobs = []
    for i in range(4):
        size = sources[i].shape[0]
        step = size // (4 if i > 1 else 1)
        for t in range(0, size, step):
            part, k = pl.ds(t, step), len(jobs)
            jobs.append(
                (
                    pltpu.make_async_copy(sources[i].at[part], held[i].at[part], sems.at[0, k]),
                    pltpu.make_async_copy(held[i].at[part], results[i].at[part], sems.at[1, k]),
                )
            )
    for first, _ in jobs:
        first.start()
    for first, second in jobs:
        first.wait()
        second.start()
    for _, second in jobs:
        second.wait()


def body(tokens, upstream, norm_gain, w_in, w_out):
    sem = pltpu.SemaphoreType.DMA
    vmem = pl.BlockSpec(memory_space=pltpu.VMEM)
    hbm = pl.BlockSpec(memory_space=pl.ANY)
    scratch = [
        pltpu.VMEM((2, 4, 2, BLK, TG), BF16),
        pltpu.VMEM((4, 2, BLK, TG), BF16),
        pltpu.VMEM((8, BLK, FB), BF16),
        pltpu.VMEM((2, FB, BLK), BF16),
        pltpu.VMEM((2, FB, BLK), BF16),
        pltpu.VMEM((2, BLK, FB), BF16),
        pltpu.VMEM((2, BLK, 128), F32),
        pltpu.VMEM((BLK, 128), F32),
        pltpu.VMEM((16, FB), F32),
        pltpu.VMEM((8, BLK), F32),
        pltpu.VMEM((3, 2, 8, TG), F32),
        pltpu.VMEM((2, 2, 8, TG), F32),
        pltpu.VMEM((8, 2, 8, TG), F32),
        pltpu.VMEM((4, 2, 8, TG), F32),
        pltpu.VMEM((2, 4, FB, TG), BF16),
        pltpu.VMEM((2, 4, FB, TG), BF16),
        pltpu.VMEM((2, FB, TG), F32),
        pltpu.VMEM((FB, TG), F32),
        pltpu.VMEM((2, 4, FB, TG), BF16),
        pltpu.VMEM((2, 4, 2, 2, 2, W, TG), BF16),
        pltpu.VMEM((2, 4, 2, 2, W, TG), BF16),
        pltpu.VMEM((2, 4, 2, 2, 2, W, TG), BF16),
        pltpu.VMEM((2, 4, 2, W, TG), BF16),
        pltpu.VMEM((W, TG), F32),
        pltpu.VMEM((2, 2, W, TG), BF16),
        pltpu.VMEM((3, 2, 8, TG), F32),
        pltpu.VMEM((2, 8, TG), F32),
        pltpu.VMEM((2, 8, TG), F32),
        pltpu.VMEM((8, 2, 8, TG), F32),
        pltpu.VMEM((1, BLK, FB), BF16),
        pltpu.VMEM((1, BLK, FB), BF16),
        pltpu.VMEM((1, FB, BLK), BF16),
        pltpu.VMEM((1, FB, BLK), BF16),
        pltpu.VMEM((BLK, FB), F32),
        pltpu.VMEM((FB, BLK), F32),
        pltpu.VMEM((W, TG), BF16),
        pltpu.VMEM((W, TG), BF16),
        sem((10,)),
        sem((2, 2)),
        sem((2, 4, 2, 2)),
        sem((2, 4, 2, 2, 2)),
        sem((2, 4, 2)),
        sem((2, 4, 2, 2)),
        sem((2, 4, 2, 2)),
        sem((2,)),
        sem((2,)),
        sem((8,)),
        sem((8,)),
        sem((4,)),
        sem((4,)),
        sem((2, 4)),
        sem((2, 4)),
        sem((2, 4)),
        sem((2, 4)),
        sem((2, 4, 2)),
        sem((2, 4, 2)),
        sem((2, 4, 2, 2)),
        sem((2, 4, 2, 2, 2)),
        sem((2, 4, 2)),
        sem((2, 4, 2)),
        sem((2, 4, 2)),
        sem((2, 2)),
        sem((2,)),
        sem((2,)),
        sem((8,)),
        sem((8,)),
        sem((2,)),
        sem((2,)),
        sem((4,)),
    ]
    shapes = (
        jax.ShapeDtypeStruct((W, TG), BF16),
        jax.ShapeDtypeStruct((W, TG), BF16),
        jax.ShapeDtypeStruct((BLK, FB), F32),
        jax.ShapeDtypeStruct((FB, BLK), F32),
    )
    results = pl.pallas_call(
        kernel,
        out_shape=shapes,
        in_specs=[vmem, vmem, vmem, hbm, hbm],
        out_specs=(hbm,) * 4,
        scratch_shapes=scratch,
        compiler_params=pltpu.CompilerParams(
            collective_id=1, has_side_effects=True, vmem_limit_bytes=58 << 20
        ),
        name="block",
    )(tokens.T, upstream.T, norm_gain, w_in, w_out)
    out_t, grad_t, grad_in, grad_out = pl.pallas_call(
        finish,
        out_shape=shapes,
        in_specs=[hbm] * 4,
        out_specs=(hbm,) * 4,
        scratch_shapes=[pltpu.VMEM(a.shape, a.dtype) for a in shapes] + [sem((2, 10))],
        name="finish",
    )(*results)
    return out_t.T, grad_t.T, grad_in, grad_out


def solution(mesh):
    return jax.shard_map(
        body,
        mesh=mesh,
        in_specs=(P("dp", "mp"), P("dp", "mp"), P(), P(None, "mp"), P("mp", None)),
        out_specs=(P("dp", "mp"), P("dp", "mp"), P("dp", "mp"), P("mp", "dp")),
        check_vma=False,
    )
```

```python
import functools

import jax
import jax.numpy as jnp
from jax import lax
from jax.experimental import pallas as pl
from jax.experimental.pallas import tpu as pltpu
from jax.sharding import PartitionSpec as P

MESH = pl.DeviceIdType.MESH
F32, BF16 = jnp.float32, jnp.bfloat16
D = 6144
BLK = 768
W = 192
TG = 256
FB = 384
ORDER = ((0, 2, 1, 3), (0, 2, 3, 1))
HG_ORDER = (1, 3, 2)
PLAN5 = ((0, 2), (1, 2), (2, 2), (3, 0), (3, 1))
PLAN6 = ((0, 2), (1, 0), (1, 1), (2, 2), (3, 0), (3, 1))
PLAN6R = ((0, 0), (0, 1), (1, 2), (2, 0), (2, 1), (3, 2))
PLAN7R = ((0, 0), (0, 1), (1, 2), (2, 0), (2, 1), (3, 0), (3, 1))
PLAN8 = tuple((t, y) for t in range(4) for y in range(2))
AG_PLAN = PLAN5
RS_PLAN = PLAN8
AG_ITEMS = len(AG_PLAN)
RS_ITEMS = len(RS_PLAN)
LAG = 2
YLAG = 2
RYLAG = 2
FILL = 4 * LAG
AG_END = 2 * AG_ITEMS + FILL
RS_START = 21
RS_END = RS_START + 2 * RS_ITEMS + FILL
LATE = 5
SLOTS = 0
ORIGIN_U = 1
BACK = ((0, 2, 4, 6), (0, 2, 4, 5))
GRAD_OUT = RS_START + 6
GRAD_IN = RS_START + 12
OWN = 4


def alone_turns(plan):
    return tuple(t for t, y in plan if y == 2)


def done(arr, turn):
    last = max(i + (YLAG if y == 2 else 0) for i, (t, y) in enumerate(AG_PLAN) if t == turn)
    return FILL + arr * AG_ITEMS + last + 1


def choose(table, i):
    value = jnp.int32(table[-1])
    for k in range(len(table) - 1):
        value = jnp.where(i == k, jnp.int32(table[k]), value)
    return value


def gelu_parts(v):
    cumul = 0.5 * (1.0 + lax.erf(v * 0.7071067811865476))
    dense = jnp.exp(-0.5 * v * v) * 0.3989422804014327
    return cumul, dense


def split_rows(row):
    n = row.shape[1]
    hi = row.astype(BF16).astype(F32)
    mid = (row - hi).astype(BF16).astype(F32)
    low = row - hi - mid
    index = lax.broadcasted_iota(jnp.int32, (16, n), 0)
    spread = [jnp.broadcast_to(v, (16, n)) for v in (hi, mid, low)]
    zero = jnp.zeros((16, n), F32)
    out = jnp.where(
        index == 0, spread[0], jnp.where(index == 1, spread[1], jnp.where(index == 2, spread[2], zero))
    )
    return out.astype(BF16)


def column(row):
    return jnp.broadcast_to(row, (128, row.shape[1])).T


def dot(a, b):
    return jnp.dot(a, b, preferred_element_type=F32)


def dot_t(a, b):
    return lax.dot_general(a, b, (((1,), (1,)), ((), ())), preferred_element_type=F32)


def kernel(
    x_ref, u_ref, gain_ref, w_in_ref, w_out_ref,
    out_ref, gt_ref, gi_ref, go_ref,
    xt, nt, wi, wit, wo, wot, gcol, gzcol, srow,
    gain8, st, stm, stz, stx, ps, pr, po, pre, hg,
    bp, br, rz, ry, acc, fin, smo, smc, smy, smz, gs, gr, gso, gro, gi_own, go_own, out_own, gt_own,
    loc_sem, org_s, ag_r, ag_z, ag_y, sib_s, sib_r, st_s, st_r, stz_s, stz_r, stx_s, stx_r, p_s, p_r, hg_s, hg_r,
    b_s, b_r, rz_s, rz_r, ry_s, ry_r, fin_s, fin_r, sm_s, sm_r, smz_s, smz_r, gr_s, gr_r, out_sem,
):
    dp, mp = lax.axis_index("dp"), lax.axis_index("mp")
    h, q = lax.div(dp, 4), lax.rem(dp, 4)
    z, yl, c = lax.div(mp, 4), lax.rem(lax.div(mp, 2), 2), lax.rem(mp, 2)

    def dev(h_, x_, z_, y_, c_):
        return (h_ * 4 + x_, z_ * 4 + y_ * 2 + c_)

    def xo(k):
        return lax.rem(q + k, 4)

    def zo(k):
        return lax.rem(z + k, 8)

    sibling = dev(h, q, z, yl, 1 - c)
    ypart = dev(h, q, z, 1 - yl, c)
    hpart = dev(1 - h, q, z, yl, c)
    zplus, zminus = dev(h, q, zo(1), yl, c), dev(h, q, zo(7), yl, c)

    def remote(src, dst, ss, rs, to):
        return pltpu.make_async_remote_copy(
            src_ref=src, dst_ref=dst, send_sem=ss, recv_sem=rs, device_id=to, device_id_type=MESH
        )

    def wi_copy(k):
        return pltpu.make_async_copy(w_in_ref.at[pl.ds(k * BLK, BLK)], wi.at[k], loc_sem.at[k])

    def wo_copy(b):
        start = pl.multiple_of((q + 4 * b) * BLK, BLK)
        return pltpu.make_async_copy(w_out_ref.at[:, pl.ds(start, BLK)], wo.at[b], loc_sem.at[8 + b])

    for k in range(8):
        wi_copy(k).start()
    for b in range(2):
        wo_copy(b).start()

    partners = [sibling, ypart, hpart]
    partners += [dev(h, q, zo(k), yl, c) for k in range(1, 8)]
    partners += [dev(h, xo(k), z, y_, c) for k in range(1, 4) for y_ in (yl, 1 - yl)]
    barrier = pltpu.get_barrier_semaphore()
    for p in partners:
        pl.semaphore_signal(barrier, inc=1, device_id=p, device_id_type=MESH)
    pl.semaphore_wait(barrier, len(partners))

    def rows(y2, cc):
        return pl.ds(pl.multiple_of(y2 * 384 + cc * W, 64), W)

    xs = lax.rem(z, 4)
    zb = lax.div(z, 4)
    mine = (x_ref, u_ref)

    def own_only(plan, k, par):
        out = k < 0
        for t in alone_turns(plan):
            out = out | (k == jnp.where(par == 1, ORDER[1][t], ORDER[0][t]))
        return out

    from_xs = lax.rem(q - xs + 4, 4)

    def origin(arr, other):
        to = dev(h, xs, z, 1 - yl if other else yl, c)
        return remote(
            mine[arr], xt.at[arr, q, zb, rows(yl, c)], org_s.at[arr, other], ag_r.at[arr, q, zb, yl], to
        )

    crosses = jnp.logical_not(own_only(AG_PLAN, from_xs, lax.rem(xs, 2)))

    def origin_sends(arr):
        pl.when(xs != q)(origin(arr, 0).start)
        pl.when(crosses)(origin(arr, 1).start)

    origin_sends(0)

    @pl.when(xs == q)
    def _():
        for arr in range(2):
            xt[arr, q, zb, rows(yl, c), :] = mine[arr][...]

    def st_copy(stage):
        return remote(st.at[stage], stm.at[stage], st_s.at[stage], st_r.at[stage], (sibling, ypart)[stage])

    def stz_copy(k):
        return remote(st.at[2], stz.at[z], stz_s.at[k], stz_r.at[z], dev(h, q, zo(k), yl, c))

    def stx_copy(k):
        return remote(stx.at[q], stx.at[q], stx_s.at[k], stx_r.at[q], dev(h, xo(k), z, yl, c))

    def own_stats():
        piece = x_ref[...].astype(F32).reshape(W // 8, 8, TG)
        total = jnp.sum(jnp.sum(piece, axis=0), axis=0, keepdims=True)
        mean = jnp.broadcast_to(total * (1.0 / W), (8, TG))
        d = piece - mean[None]
        st[0, 0] = mean
        spread = jnp.sum(jnp.sum(d * d, axis=0), axis=0, keepdims=True)
        st[0, 1] = jnp.broadcast_to(spread, (8, TG))
        st_copy(0).start()

    def merge(parts, count):
        mean = sum(p[0] for p in parts) * (1.0 / len(parts))
        spread = sum(p[1] for p in parts)
        for p in parts:
            spread = spread + (p[0] - mean) * (p[0] - mean) * float(count)
        return mean, spread

    def merge_pair(stage):
        st_copy(stage).wait_recv()
        parts = [(st[stage, 0], st[stage, 1]), (stm[stage, 0], stm[stage, 1])]
        st[stage + 1, 0], st[stage + 1, 1] = merge(parts, W * (stage + 1))
        if stage == 0:
            st_copy(1).start()
        else:
            for k in range(1, 8):
                stz_copy(k).start()

    def merge_z():
        parts = [(st[2, 0], st[2, 1])]
        for k in range(1, 8):
            other = stz.at[zo(k)]
            remote(other, other, stz_s.at[k], stz_r.at[zo(k)], sibling).wait_recv()
            parts.append((stz[zo(k), 0], stz[zo(k), 1]))
        mean, spread = merge(parts, 4 * W)
        stx[q, 0] = mean
        stx[q, 1] = lax.rsqrt(spread / D + 1e-06)
        for k in range(1, 4):
            stx_copy(k).start()

    own_stats()

    odd = lax.rem(q, 2)

    def offset(turn):
        off = [jnp.where(odd == 1, ORDER[1][i], ORDER[0][i]) for i in range(4)]
        if isinstance(turn, int):
            return off[turn]
        return jnp.where(turn < 2, jnp.where(turn == 0, off[0], off[1]), jnp.where(turn == 2, off[2], off[3]))

    def item(n, plan):
        arr, m = lax.div(n, len(plan)), lax.rem(n, len(plan))
        half = choose([y for _, y in plan], m)
        alone = half == 2
        k = offset(choose([t for t, _ in plan], m))
        return arr, xo(k), jnp.where(alone, yl, half), alone

    def place(b):
        rb = lax.rem(z - q + 8 - 4 * b, 8)
        return rb, jnp.minimum(rb, 8 - rb)

    def sib_copy(arr, g, b, y2, cc):
        piece = xt.at[arr, g, b, rows(y2, cc)]
        return remote(piece, piece, sib_s.at[arr, g, b, y2], sib_r.at[arr, g, b, y2], sibling)

    def ag_copies(b, rb, n):
        arr, g, y2, alone = item(n, AG_PLAN)
        piece = xt.at[arr, g, b, rows(y2, c)]
        recv = ag_r.at[arr, g, b, y2]
        up = (rb <= 2) | ((rb == 3) & (y2 == 0))
        down = (rb == 0) | (rb >= 6) | ((rb == 5) & (y2 == 1))
        local = (rb == 0) & (g == q) & (y2 == yl)
        c_up = remote(piece, piece, ag_z.at[arr, g, b, y2, 0], recv, zplus)
        c_down = remote(piece, piece, ag_z.at[arr, g, b, y2, 1], recv, zminus)
        c_y = remote(piece, piece, ag_y.at[arr, g, b], recv, ypart)
        return up, down, local, alone, c_up, c_down, c_y, sib_copy(arr, g, b, y2, c)

    def ag_step(s):
        for b in range(2):
            rb, dist = place(b)
            n = s - LAG * dist

            @pl.when((n >= 0) & (n < 2 * AG_ITEMS))
            def _():
                up, down, local, alone, c_up, c_down, c_y, c_sib = ag_copies(b, rb, n)

                @pl.when(jnp.logical_not(local))
                def _():
                    c_up.wait_recv()

                c_sib.start()
                pl.when(up)(c_up.start)
                pl.when(down)(c_down.start)
                pl.when(alone)(c_y.start)

        for b in range(2):
            _, dist = place(b)
            late = s - LAG * dist - YLAG

            @pl.when((late >= 0) & (late < 2 * AG_ITEMS))
            def _():
                arr, g, _, alone = item(late, AG_PLAN)

                @pl.when(alone)
                def _():
                    c_sib = sib_copy(arr, g, b, 1 - yl, c)
                    piece = xt.at[arr, g, b, rows(1 - yl, c)]
                    remote(piece, piece, ag_y.at[arr, g, b], ag_r.at[arr, g, b, 1 - yl], ypart).wait_recv()
                    c_sib.start()

    def prep_wi(b):
        for k in range(4 * b, 4 * b + 4):
            wi_copy(k).wait()

    def prep_s(lo, hi):
        for k in range(lo, hi):
            term = dot(split_rows(gain8[k : k + 1, :]), wi[k])
            if k == 0:
                srow[...] = term
            else:
                srow[...] += term

    def prep_wit(b):
        for t in range(2):
            part = wi[q + 4 * b, pl.ds(t * 384, 384), :]
            wit[b, :, t * 384 : (t + 1) * 384] = part.T

    def prep_wot(b):
        wo_copy(b).wait()
        for t in range(2):
            wot[b, t * 384 : (t + 1) * 384, :] = wo[b, :, t * 384 : (t + 1) * 384].T

    def prep_gain():
        for k in range(8):
            gain8[k : k + 1, :] = gain_ref[k * BLK : (k + 1) * BLK].reshape(1, BLK)
        for b in range(2):
            gcol[b] = column(gain8[pl.ds(q + 4 * b, 1), :])
        gzcol[...] = column(gain8[pl.ds(z, 1), :])

    def wait_sib(arr, g):
        for b in range(2):
            for y2 in range(2):
                sib_copy(arr, g, b, y2, 1 - c).wait_recv()

    def p_copy(arr, k):
        return remote(ps.at[arr, xo(k)], pr.at[arr, q], p_s.at[arr, k], p_r.at[arr, q], dev(h, xo(k), z, yl, c))

    def put_part(arr, k, part):
        @pl.when(k == 0)
        def _():
            po[arr] = part

        @pl.when(k > 0)
        def _():
            ps[arr, xo(k)] = part.astype(BF16)
            p_copy(arr, k).start()

    def norm_part(turn):
        k = offset(turn)
        g = xo(k)
        wait_sib(0, g)

        @pl.when(k > 0)
        def _():
            other = stx.at[g]
            remote(other, other, stx_s.at[k], stx_r.at[g], sibling).wait_recv()

        mean, inv = stx[g, 0], stx[g, 1]

        def scale(i, _):
            b = lax.div(i, 4)
            r = pl.ds(pl.multiple_of(lax.rem(i, 4) * W, 64), W)
            piece = xt[0, g, b, r, :].astype(F32).reshape(W // 8, 8, TG)
            unit = ((piece - mean[None]) * inv[None]).reshape(W, TG)
            gain = gcol[b, r, :]
            nt[g, b, r, :] = (unit * jnp.concatenate([gain, gain], axis=1)).astype(BF16)
            return 0

        lax.fori_loop(0, 8, scale, 0)
        put_part(0, k, dot(wit[0], nt[g, 0]) + dot(wit[1], nt[g, 1]))

    def up_part(turn):
        k = offset(turn)
        g = xo(k)
        wait_sib(1, g)
        put_part(1, k, dot(wo[0], xt[1, g, 0]) + dot(wo[1], xt[1, g, 1]))

    def summed(arr):
        total = po[arr]
        for k in range(1, 4):
            other = pr.at[arr, xo(k)]
            remote(other, other, p_s.at[arr, k], p_r.at[arr, xo(k)], sibling).wait_recv()
            total = total + pr[arr, xo(k)].astype(F32)
        return total

    def hg_copy(arr, k):
        return remote(hg.at[arr, q], hg.at[arr, q], hg_s.at[arr, k], hg_r.at[arr, q], dev(h, xo(k), z, yl, c))

    def last_h():
        preact = summed(0)
        pre[...] = preact
        cumul, _ = gelu_parts(preact)
        hg[0, q] = (preact * cumul).astype(BF16)
        for k in HG_ORDER:
            hg_copy(0, k).start()

    def sm_copy(stage):
        dst, to = ((smc, sibling), (smy, ypart))[stage]
        return remote(smo.at[stage], dst, sm_s.at[stage], sm_r.at[stage], to)

    def smz_copy(k):
        return remote(smo.at[2], smz.at[z], smz_s.at[k], smz_r.at[z], dev(h, q, zo(k), yl, c))

    def last_g():
        grad_hidden = summed(1)
        preact = pre[...]
        cumul, dense = gelu_parts(preact)
        grad = (grad_hidden * (cumul + preact * dense)).astype(BF16)
        hg[1, q] = grad
        for k in HG_ORDER:
            hg_copy(1, k).start()
        by_gain = split_rows(jnp.sum(srow[...], axis=0, keepdims=True))
        smo[0, 0] = jnp.broadcast_to(jnp.sum(dot(by_gain, grad), axis=0, keepdims=True), (8, TG))
        inner = jnp.sum(grad.astype(F32) * preact, axis=0, keepdims=True)
        smo[0, 1] = jnp.broadcast_to(inner, (8, TG))
        sm_copy(0).start()

    def finish_h(slot):
        pl.when(odd == slot)(last_h)

    def finish_g(slot):
        pl.when(odd == slot)(last_g)

    def small_1():
        sm_copy(0).wait_recv()
        smo[1] = smo[0] + smc[...]
        sm_copy(1).start()

    def small_2():
        sm_copy(1).wait_recv()
        smo[2] = smo[1] + smy[...]
        for k in range(1, 8):
            smz_copy(k).start()

    def b_copy(arr, g, b):
        return remote(bp.at[arr, g, b, 1 - c], br.at[arr, g, b], b_s.at[arr, g, b], b_r.at[arr, g, b], sibling)

    def back_part(arr, turn):
        k = offset(turn)
        g = xo(k)

        @pl.when(k > 0)
        def _():
            other = hg.at[arr, g]
            remote(other, other, hg_s.at[arr, k], hg_r.at[arr, g], sibling).wait_recv()
        act = hg[arr, g]
        for b in range(2):
            for y2 in range(2):
                w = wot[b, y2 * 384 : (y2 + 1) * 384, :] if arr == 0 else wi[q + 4 * b, pl.ds(y2 * 384, 384), :]
                part = dot(w, act).astype(BF16)
                bp[arr, g, b, 0, y2] = part[:W]
                bp[arr, g, b, 1, y2] = part[W:]
            b_copy(arr, g, b).start()

    def rs_flags(rb, g, y2):
        from_up = (rb <= 2) | ((rb == 3) & (y2 == 0))
        from_down = (rb == 0) | (rb >= 6) | ((rb == 5) & (y2 == 1))
        to_down = ((rb >= 1) & (rb <= 3)) | ((rb == 4) & (y2 == 0))
        to_up = (rb >= 5) | ((rb == 4) & (y2 == 1))
        sink = rb == 0
        local = sink & (g == q) & (y2 == yl)
        return from_up, from_down, to_up, to_down, sink, local

    def rs_copies(b, arr, g, y2):
        piece = bp.at[arr, g, b, c, y2]
        sent, got = rz_s.at[arr, g, b, y2], rz_r.at[arr, g, b, y2]
        c_down = remote(piece, rz.at[arr, g, b, y2, 0], sent, got.at[0], zminus)
        c_up = remote(piece, rz.at[arr, g, b, y2, 1], sent, got.at[1], zplus)
        c_fin = remote(piece, fin.at[arr, yl], fin_s.at[arr, g, y2], fin_r.at[arr, yl], dev(h, g, z, y2, c))
        return c_up, c_down, c_fin

    def ry_copy(arr, g, b):
        return remote(bp.at[arr, g, b, c, 1 - yl], ry.at[arr, g, b], ry_s.at[arr, g, b], ry_r.at[arr, g, b], ypart)

    def rs_step(s):
        for b in range(2):
            rb, dist = place(b)
            n = s - LAG * (4 - dist)
            early = n + RYLAG

            @pl.when((early >= 0) & (early < 2 * RS_ITEMS))
            def _():
                arr, g, _, alone = item(early, RS_PLAN)

                @pl.when(alone)
                def _():
                    b_copy(arr, g, b).wait_recv()
                    both = bp[arr, g, b, c, 1 - yl].astype(F32) + br[arr, g, b, 1 - yl].astype(F32)
                    bp[arr, g, b, c, 1 - yl] = both.astype(BF16)
                    ry_copy(arr, g, b).start()

            @pl.when((n >= 0) & (n < 2 * RS_ITEMS))
            def _():
                arr, g, y2, alone = item(n, RS_PLAN)
                from_up, from_down, to_up, to_down, sink, local = rs_flags(rb, g, y2)
                c_up, c_down, c_fin = rs_copies(b, arr, g, y2)

                @pl.when((y2 == 0) & jnp.logical_not(alone))
                def _():
                    b_copy(arr, g, b).wait_recv()

                acc[...] = bp[arr, g, b, c, y2].astype(F32) + br[arr, g, b, y2].astype(F32)

                @pl.when(alone)
                def _():
                    ry_copy(arr, g, b).wait_recv()
                    acc[...] += ry[arr, g, b].astype(F32)

                @pl.when(from_up)
                def _():
                    c_down.wait_recv()
                    acc[...] += rz[arr, g, b, y2, 0].astype(F32)

                @pl.when(from_down)
                def _():
                    c_up.wait_recv()
                    acc[...] += rz[arr, g, b, y2, 1].astype(F32)

                bp[arr, g, b, c, y2] = acc[...].astype(BF16)
                pl.when(to_up)(c_up.start)
                pl.when(to_down)(c_down.start)
                pl.when(sink & jnp.logical_not(local))(c_fin.start)

                @pl.when(local)
                def _():
                    fin[arr, yl] = acc[...].astype(BF16)

    def gr_copy(i):
        return remote((gs, gso)[i].at[0], (gr, gro)[i].at[0], gr_s.at[i], gr_r.at[i], hpart)

    def grad_out_sent():
        for t in range(2):
            other = sum(dot_t(hg[0, g], xt[1, g, 1 - h, pl.ds(t * 384, 384), :]) for g in range(4))
            gso[0, :, t * 384 : (t + 1) * 384] = other.astype(BF16)
        gr_copy(1).start()

    def grad_out_own():
        for t in range(2):
            go_own[:, t * 384 : (t + 1) * 384] = sum(
                dot_t(hg[0, g], xt[1, g, h, pl.ds(t * 384, 384), :]) for g in range(4)
            )

    def grad_in_sent():
        for t in range(2):
            other = sum(dot_t(nt[g, 1 - h, pl.ds(t * 384, 384), :], hg[1, g]) for g in range(4))
            gs[0, t * 384 : (t + 1) * 384, :] = other.astype(BF16)
        gr_copy(0).start()

    def grad_in_own():
        for t in range(2):
            gi_own[t * 384 : (t + 1) * 384, :] = sum(
                dot_t(nt[g, h, pl.ds(t * 384, 384), :], hg[1, g]) for g in range(4)
            )

    turns = {}

    def at(step, run, *args):
        turns.setdefault(step, []).append(functools.partial(run, *args))

    at(1, merge_pair, 0)
    at(1, prep_wi, 0)
    at(2, prep_wi, 1)
    at(2, prep_gain)
    at(3, merge_pair, 1)
    for b in range(2):
        at(3 + b, prep_wit, b)
        at(6 + b, prep_wot, b)
        at(8 + b, prep_s, 4 * b, 4 * b + 4)
    at(5, merge_z)
    at(ORIGIN_U, origin_sends, 1)
    for i in range(4):
        at(done(0, i), norm_part, i)
        at(done(1, i), up_part, i)
        for arr in range(2):
            at(RS_START + RS_ITEMS * arr - 1 + BACK[arr][i], back_part, arr, i)
    for slot in range(2):
        last = (2 * slot, 2 * slot + 1) if SLOTS else range(4)
        at(max(done(0, i) for i in last) + LATE, finish_h, slot)
        at(max(done(1, i) for i in last) + LATE, finish_g, slot)
    at(GRAD_OUT, grad_out_sent)
    at(RS_END - OWN, grad_out_own)
    at(max(done(1, 2), done(1, 3)) + LATE + 2, small_1)
    at(max(done(1, 2), done(1, 3)) + LATE + 4, small_2)
    at(GRAD_IN, grad_in_sent)
    at(RS_END - OWN + 1, grad_in_own)

    def both(s, _):
        ag_step(s)
        rs_step(s - RS_START)
        return 0

    def first(s, _):
        ag_step(s)
        return 0

    def second(s, _):
        rs_step(s - RS_START)
        return 0

    marks = sorted(set(turns) | {0, RS_START - 2, AG_END, RS_END})
    for lo, hi in zip(marks, marks[1:] + [RS_END]):
        for run in turns.get(lo, ()):
            run()
        if lo < hi:
            lax.fori_loop(lo, hi, first if lo < RS_START - 2 else both if lo < AG_END else second, 0)

    outs = ((gi_own, gi_ref), (go_own, go_ref), (out_own, out_ref), (gt_own, gt_ref))

    def put(i):
        return pltpu.make_async_copy(outs[i][0], outs[i][1], out_sem.at[i])

    gr_copy(1).wait_recv()
    go_own[...] += gro[0].astype(F32)
    put(1).start()
    gr_copy(0).wait_recv()
    gi_own[...] += gr[0].astype(F32)
    put(0).start()

    for arr in range(2):
        pl.when(xs != q)(origin(arr, 0).wait_send)
        pl.when(crosses)(origin(arr, 1).wait_send)
        for k in range(1, 4):
            hg_copy(arr, k).wait_send()
            p_copy(arr, k).wait_send()
    for i in range(2):
        gr_copy(i).wait_send()
        sm_copy(i).wait_send()
    for k in range(1, 8):
        smz_copy(k).wait_send()

    def drain_ag(n, _):
        for b in range(2):
            rb, _ = place(b)
            up, down, _, alone, c_up, c_down, c_y, c_sib = ag_copies(b, rb, n)
            arr, g, _, _ = item(n, AG_PLAN)
            pl.when(up)(c_up.wait_send)
            pl.when(down)(c_down.wait_send)
            c_sib.wait_send()

            @pl.when(alone)
            def _():
                c_y.wait_send()
                sib_copy(arr, g, b, 1 - yl, c).wait_send()

        return 0

    def drain_rs(n, _):
        for b in range(2):
            rb, _ = place(b)
            arr, g, y2, alone = item(n, RS_PLAN)
            _, _, to_up, to_down, sink, local = rs_flags(rb, g, y2)
            c_up, c_down, c_fin = rs_copies(b, arr, g, y2)
            pl.when(to_up)(c_up.wait_send)
            pl.when(to_down)(c_down.wait_send)
            pl.when(sink & jnp.logical_not(local))(c_fin.wait_send)
            pl.when(alone)(ry_copy(arr, g, b).wait_send)
            pl.when((y2 == 0) | alone)(b_copy(arr, g, b).wait_send)
        return 0

    lax.fori_loop(0, 2 * AG_ITEMS, drain_ag, 0)
    lax.fori_loop(0, 2 * RS_ITEMS, drain_rs, 0)

    for k in range(1, 8):
        stz_copy(k).wait_send()
    for k in range(1, 4):
        stx_copy(k).wait_send()
    for i in range(2):
        st_copy(i).wait_send()

    alone = own_only(RS_PLAN, from_xs, lax.rem(xs, 2))

    def fin_wait(arr):
        @pl.when(alone)
        def _():
            fin[arr, 1 - yl] = jnp.zeros((W, TG), BF16)

        for y2 in range(2):

            @pl.when(jnp.logical_not((xs == q) & (yl == y2)) & ((yl == y2) | jnp.logical_not(alone)))
            def _():
                piece = fin.at[arr, y2]
                remote(piece, piece, fin_s.at[arr, 0, y2], fin_r.at[arr, y2], sibling).wait_recv()

    fin_wait(0)
    out_own[...] = (x_ref[...].astype(F32) + (fin[0, 0].astype(F32) + fin[0, 1].astype(F32))).astype(BF16)

    sums = smo[2]
    for k in range(1, 8):
        remote(smz.at[zo(k)], smz.at[zo(k)], smz_s.at[k], smz_r.at[zo(k)], sibling).wait_recv()
        sums = sums + smz[zo(k)]
    mean, inv = stx[q, 0][None], stx[q, 1][None]
    unit = (x_ref[...].astype(F32).reshape(W // 8, 8, TG) - mean) * inv
    gain = gzcol[rows(yl, c), :]
    gain = jnp.concatenate([gain, gain], axis=1)
    fin_wait(1)
    scaled = ((fin[1, 0].astype(F32) + fin[1, 1].astype(F32)) * gain).reshape(W // 8, 8, TG)
    grad_ln = inv * (scaled - (sums[0] / D)[None] - unit * (sums[1] / D)[None])
    put(2).start()
    gt_own[...] = (u_ref[...].astype(F32) + grad_ln.reshape(W, TG)).astype(BF16)


    put(3).start()

    for i in range(4):
        put(i).wait()


def finish(*refs):
    sources, results, held, sems = refs[:4], refs[4:8], refs[8:12], refs[12]
    jobs = []
    for i in range(4):
        size = sources[i].shape[0]
        step = size // (4 if i > 1 else 1)
        for t in range(0, size, step):
            part, k = pl.ds(t, step), len(jobs)
            jobs.append(
                (
                    pltpu.make_async_copy(sources[i].at[part], held[i].at[part], sems.at[0, k]),
                    pltpu.make_async_copy(held[i].at[part], results[i].at[part], sems.at[1, k]),
                )
            )
    for first, _ in jobs:
        first.start()
    for first, second in jobs:
        first.wait()
        second.start()
    for _, second in jobs:
        second.wait()


def body(tokens, upstream, norm_gain, w_in, w_out):
    sem = pltpu.SemaphoreType.DMA
    vmem = pl.BlockSpec(memory_space=pltpu.VMEM)
    hbm = pl.BlockSpec(memory_space=pl.ANY)
    scratch = [
        pltpu.VMEM((2, 4, 2, BLK, TG), BF16),
        pltpu.VMEM((4, 2, BLK, TG), BF16),
        pltpu.VMEM((8, BLK, FB), BF16),
        pltpu.VMEM((2, FB, BLK), BF16),
        pltpu.VMEM((2, FB, BLK), BF16),
        pltpu.VMEM((2, BLK, FB), BF16),
        pltpu.VMEM((2, BLK, 128), F32),
        pltpu.VMEM((BLK, 128), F32),
        pltpu.VMEM((16, FB), F32),
        pltpu.VMEM((8, BLK), F32),
        pltpu.VMEM((3, 2, 8, TG), F32),
        pltpu.VMEM((2, 2, 8, TG), F32),
        pltpu.VMEM((8, 2, 8, TG), F32),
        pltpu.VMEM((4, 2, 8, TG), F32),
        pltpu.VMEM((2, 4, FB, TG), BF16),
        pltpu.VMEM((2, 4, FB, TG), BF16),
        pltpu.VMEM((2, FB, TG), F32),
        pltpu.VMEM((FB, TG), F32),
        pltpu.VMEM((2, 4, FB, TG), BF16),
        pltpu.VMEM((2, 4, 2, 2, 2, W, TG), BF16),
        pltpu.VMEM((2, 4, 2, 2, W, TG), BF16),
        pltpu.VMEM((2, 4, 2, 2, 2, W, TG), BF16),
        pltpu.VMEM((2, 4, 2, W, TG), BF16),
        pltpu.VMEM((W, TG), F32),
        pltpu.VMEM((2, 2, W, TG), BF16),
        pltpu.VMEM((3, 2, 8, TG), F32),
        pltpu.VMEM((2, 8, TG), F32),
        pltpu.VMEM((2, 8, TG), F32),
        pltpu.VMEM((8, 2, 8, TG), F32),
        pltpu.VMEM((1, BLK, FB), BF16),
        pltpu.VMEM((1, BLK, FB), BF16),
        pltpu.VMEM((1, FB, BLK), BF16),
        pltpu.VMEM((1, FB, BLK), BF16),
        pltpu.VMEM((BLK, FB), F32),
        pltpu.VMEM((FB, BLK), F32),
        pltpu.VMEM((W, TG), BF16),
        pltpu.VMEM((W, TG), BF16),
        sem((10,)),
        sem((2, 2)),
        sem((2, 4, 2, 2)),
        sem((2, 4, 2, 2, 2)),
        sem((2, 4, 2)),
        sem((2, 4, 2, 2)),
        sem((2, 4, 2, 2)),
        sem((2,)),
        sem((2,)),
        sem((8,)),
        sem((8,)),
        sem((4,)),
        sem((4,)),
        sem((2, 4)),
        sem((2, 4)),
        sem((2, 4)),
        sem((2, 4)),
        sem((2, 4, 2)),
        sem((2, 4, 2)),
        sem((2, 4, 2, 2)),
        sem((2, 4, 2, 2, 2)),
        sem((2, 4, 2)),
        sem((2, 4, 2)),
        sem((2, 4, 2)),
        sem((2, 2)),
        sem((2,)),
        sem((2,)),
        sem((8,)),
        sem((8,)),
        sem((2,)),
        sem((2,)),
        sem((4,)),
    ]
    shapes = (
        jax.ShapeDtypeStruct((W, TG), BF16),
        jax.ShapeDtypeStruct((W, TG), BF16),
        jax.ShapeDtypeStruct((BLK, FB), F32),
        jax.ShapeDtypeStruct((FB, BLK), F32),
    )
    results = pl.pallas_call(
        kernel,
        out_shape=shapes,
        in_specs=[vmem, vmem, vmem, hbm, hbm],
        out_specs=(hbm,) * 4,
        scratch_shapes=scratch,
        compiler_params=pltpu.CompilerParams(
            collective_id=1, has_side_effects=True, vmem_limit_bytes=58 << 20
        ),
        name="block",
    )(tokens.T, upstream.T, norm_gain, w_in, w_out)
    out_t, grad_t, grad_in, grad_out = pl.pallas_call(
        finish,
        out_shape=shapes,
        in_specs=[hbm] * 4,
        out_specs=(hbm,) * 4,
        scratch_shapes=[pltpu.VMEM(a.shape, a.dtype) for a in shapes] + [sem((2, 10))],
        name="finish",
    )(*results)
    return out_t.T, grad_t.T, grad_in, grad_out


def solution(mesh):
    return jax.shard_map(
        body,
        mesh=mesh,
        in_specs=(P("dp", "mp"), P("dp", "mp"), P(), P(None, "mp"), P("mp", None)),
        out_specs=(P("dp", "mp"), P("dp", "mp"), P("dp", "mp"), P("mp", "dp")),
        check_vma=False,
    )
```
